512 devices in a mesh: seq: 64 (over z_lo, y, core), tensor: 8 (over z_hi, x).
Axes of the slice: x: 4, y: 4, z: 16 (z_hi: 2, z_lo: 8; z = z_hi * 8 + z_lo), core: 2. Of those that a mesh axis runs over, the one named last changes fastest.
Arguments:
- queries: bfloat16 [16384, 4096], P('seq', 'tensor'), may hold values from -9 to 9
- key_rows: bfloat16 [16384, 1024], P('seq', 'tensor'), may hold values from -9 to 9
- value_rows: bfloat16 [16384, 1024], P('seq', 'tensor'), may hold values from -6 to 6
- out_weight: bfloat16 [4096, 4096], P(('tensor', 'seq')), may hold values from -0.09375 to 0.09375
- out_grad: bfloat16 [16384, 4096], P('seq', 'tensor'), may hold values from -6 to 6
- doc_lengths: int32 [128], replicated, may hold values from 1 to 1024, 16384 in all
Outputs:
- attn_out: bfloat16 [16384, 4096], P('seq', 'tensor')
- grad_queries: bfloat16 [16384, 4096], P('seq', 'tensor')
- grad_keys: bfloat16 [16384, 1024], P('seq', 'tensor')
- grad_values: bfloat16 [16384, 1024], P('seq', 'tensor')
The draws below stay inside these ranges and needn't reach their ends.
Inputs may be any that keep to these rules, and one draw needn't show every extreme that they name: `doc_lengths`: the lengths sum to 16384; the longest is exactly 1024.
All inputs are finite; a program needn't handle non-finite values.
Results may differ from the reference program's by a relative error of at most 0.025.
Values may be sent and summed in bfloat16 or wider, within the bound.
A program may use at most 64 MiB of HBM per device.

```python
import math
import jax
import jax.numpy as jnp
import numpy as np
from jax import lax

D = 4096
HQ = 32
HK = 8
DH = 128
TOK_DEV = 256
SPAN = 4
TOKENS = 16384
DOCS = 128
N_TENSOR = 8


def draw_queries(key, part):
    key = jax.random.fold_in(key, 11)
    return jnp.clip(jax.random.normal(key, (TOKENS, HQ * DH), jnp.float32), -6.0, 6.0).astype(jnp.bfloat16)


def draw_key_rows(key, part):
    key = jax.random.fold_in(key, 12)
    return jnp.clip(jax.random.normal(key, (TOKENS, HK * DH), jnp.float32), -6.0, 6.0).astype(jnp.bfloat16)


def block_scale(stream_key, shape, cuts, smallest, high):
    loudness, own = 1.0, jax.random.fold_in(stream_key, 6)
    for position, shards_of in cuts:
        heights = jnp.exp(jax.random.uniform(jax.random.fold_in(own, position), (shards_of,), jnp.float32, smallest / len(cuts), high / len(cuts)))
        loudness = loudness * jnp.repeat(heights, shape[position] // shards_of).reshape([-1 if axis == position else 1 for axis in range(len(shape))])
    return loudness


def profile(number_of, total, limit, skew):
    loads = [(1 << 20) // math.isqrt(rank ** skew) + 1 for rank in range(2, number_of + 1)]
    surplus, counts = total - limit - (number_of - 1), [1] * (number_of - 1)
    while surplus > 0:
        free = [i for i in range(number_of - 1) if counts[i] < limit]
        pool, left = sum([loads[i] for i in free]), surplus
        for i in free:
            extra = min(limit - counts[i], max(1, left * loads[i] // pool), surplus)
            counts[i] = counts[i] + extra
            surplus = surplus - extra
    return np.array([limit] + counts)


def ragged_sizes(key, count, total, reach, lean):
    if count == 2:
        one = jax.random.randint(key, (), max(1, total - reach), min(reach, total - 1) + 1)
        return jnp.stack([one, total - one])
    sizes = jnp.asarray(profile(count, total, reach, lean), jnp.int32)
    couples = (count - 1) // 2
    donor, taker = sizes[1:1 + 2 * couples:2], sizes[2:2 + 2 * couples:2]
    margin = jnp.minimum(donor - 1, reach - taker)
    shifted = jax.random.randint(jax.random.fold_in(key, 1), (couples,), 0, 1 << 20) % (margin + 1)
    sizes = sizes.at[1:1 + 2 * couples:2].set(donor - shifted).at[2:2 + 2 * couples:2].set(taker + shifted)
    return sizes[jax.random.permutation(jax.random.fold_in(key, 2), count)]


def centred(rng, shape, scale, most, pieces=(), kind=jnp.bfloat16):
    drawn = jax.random.normal(rng, shape, jnp.float32) * scale
    if len(pieces) > 0:
        drawn = block_scale(rng, shape, pieces, -0.22, 0.18) * drawn
    return jnp.clip(drawn, min=-most, max=most).astype(kind)


def setup_inputs(seed: int = 0) -> dict:
    key_list = jax.random.split(jax.random.key(seed), 7)
    queries = draw_queries(jax.random.fold_in(key_list[6], 71), 0)
    key_rows = draw_key_rows(jax.random.fold_in(key_list[6], 71), 0)
    value_rows = centred(key_list[2], (TOKENS, HK * DH), 1.0, 6.0, ((0, 64), (1, 8)))
    out_weight = centred(key_list[3], (HQ * DH, D), (HQ * DH) ** -0.5, 0.09375, ((0, 512),))
    out_grad = centred(key_list[4], (TOKENS, D), 1.0, 6.0, ((0, 64), (1, 8)))
    doc_lengths = ragged_sizes(key_list[5], DOCS, TOKENS, SPAN * TOK_DEV, 2).astype(jnp.int32)
    return {"queries": queries, "key_rows": key_rows, "value_rows": value_rows, "out_weight": out_weight, "out_grad": out_grad, "doc_lengths": doc_lengths}


NEG_FILL = -1e+30

def doc_index(positions, doc_lengths):
    doc_ends = jnp.cumsum(doc_lengths).astype(jnp.int32)
    counted = lax.optimization_barrier(jnp.sum((doc_ends[None, :] <= positions[:, None]).astype(jnp.int32), axis=1)).astype(jnp.int32)
    return jnp.where(positions < 0, -1, counted).astype(jnp.int32)

def reference(queries, key_rows, value_rows, out_weight, out_grad, doc_lengths):
    score_scale = 1.0 / math.sqrt(DH)
    group_size = HQ // HK
    window = (SPAN + 1) * TOK_DEV
    block_count = TOKENS // TOK_DEV
    pad_rows = SPAN * TOK_DEV
    query_heads = queries.reshape(TOKENS, HK, group_size, DH)
    keys_padded = jnp.concatenate([jnp.zeros((pad_rows, HK, DH), jnp.bfloat16), key_rows.reshape(TOKENS, HK, DH)], axis=0)
    values_padded = jnp.concatenate([jnp.zeros((pad_rows, HK, DH), jnp.bfloat16), value_rows.reshape(TOKENS, HK, DH)], axis=0)
    block_ids = jnp.arange(block_count, dtype=jnp.int32)

    def window_parts(block_id):
        first_row = (block_id * TOK_DEV).astype(jnp.int32)
        query_block = lax.dynamic_slice_in_dim(query_heads, first_row, TOK_DEV, 0)
        key_window = lax.dynamic_slice_in_dim(keys_padded, first_row, window, 0)
        value_window = lax.dynamic_slice_in_dim(values_padded, first_row, window, 0)
        query_index = first_row + jnp.arange(TOK_DEV, dtype=jnp.int32)
        key_index = first_row - pad_rows + jnp.arange(window, dtype=jnp.int32)
        visible = (doc_index(query_index, doc_lengths)[:, None] == doc_index(key_index, doc_lengths)[None, :]) & (key_index[None, :] <= query_index[:, None])
        scores = jnp.einsum('rkgd,wkd->kgrw', query_block.astype(jnp.float32), key_window.astype(jnp.float32)) * score_scale
        scores = jnp.where(visible[None, None], scores, NEG_FILL)
        return (query_block, key_window, value_window, visible, scores)

    def forward_block(block_id):
        query_block, key_window, value_window, visible, scores = window_parts(block_id)
        block_top = lax.optimization_barrier(jnp.max(scores, axis=3, keepdims=True))
        block_total = lax.optimization_barrier(jnp.sum(jnp.where(visible[None, None], jnp.exp(scores - block_top), 0.0), axis=3, keepdims=True))
        log_total = block_top + jnp.log(block_total)
        weights = jnp.where(visible[None, None], jnp.exp(scores - log_total), 0.0).astype(jnp.bfloat16)
        context = jnp.einsum('kgrw,wkd->rkgd', weights.astype(jnp.float32), value_window.astype(jnp.float32)).astype(jnp.bfloat16)
        return (context, log_total[..., 0])
    contexts, log_totals = lax.map(forward_block, block_ids)
    context_flat = contexts.reshape(TOKENS, HQ * DH)
    slab_rows = HQ * DH // N_TENSOR
    attn_sum = jnp.zeros((TOKENS, D), jnp.float32)
    for member in range(N_TENSOR):
        partial_value = jnp.dot(context_flat[:, member * slab_rows:(member + 1) * slab_rows], out_weight[member * slab_rows:(member + 1) * slab_rows], preferred_element_type=jnp.float32)
        attn_sum = attn_sum + lax.optimization_barrier(partial_value.astype(jnp.bfloat16)).astype(jnp.float32)
    attn_out = attn_sum.astype(jnp.bfloat16)
    grad_context = jnp.dot(out_grad, out_weight.T, preferred_element_type=jnp.float32).astype(jnp.bfloat16)
    grad_heads = grad_context.reshape(TOKENS, HK, group_size, DH)
    context_heads = contexts.reshape(TOKENS, HK, group_size, DH)
    delta_all = lax.optimization_barrier(jnp.sum(grad_heads.astype(jnp.float32) * context_heads.astype(jnp.float32), axis=3))

    def backward_block(carried, block_id):
        key_acc, value_acc = carried
        query_block, key_window, value_window, visible, scores = window_parts(block_id)
        first_row = (block_id * TOK_DEV).astype(jnp.int32)
        grad_block = lax.dynamic_slice_in_dim(grad_heads, first_row, TOK_DEV, 0)
        delta_block = jnp.transpose(lax.dynamic_slice_in_dim(delta_all, first_row, TOK_DEV, 0), (1, 2, 0))
        log_block = lax.dynamic_index_in_dim(log_totals, block_id, 0, keepdims=False)
        probabilities = jnp.where(visible[None, None], jnp.exp(scores - log_block[..., None]), 0.0)
        weights = probabilities.astype(jnp.bfloat16)
        prob_grad = jnp.einsum('rkgd,wkd->kgrw', grad_block.astype(jnp.float32), value_window.astype(jnp.float32))
        score_grad = (probabilities * (prob_grad - delta_block[..., None])).astype(jnp.bfloat16)
        query_part = jnp.einsum('kgrw,wkd->rkgd', score_grad.astype(jnp.float32), key_window.astype(jnp.float32))
        key_part = jnp.einsum('kgrw,rkgd->wkd', score_grad.astype(jnp.float32), query_block.astype(jnp.float32))
        value_part = jnp.einsum('kgrw,rkgd->wkd', weights.astype(jnp.float32), grad_block.astype(jnp.float32))
        key_acc = lax.dynamic_update_slice_in_dim(key_acc, lax.dynamic_slice_in_dim(key_acc, first_row, window, 0) + key_part, first_row, 0)
        value_acc = lax.dynamic_update_slice_in_dim(value_acc, lax.dynamic_slice_in_dim(value_acc, first_row, window, 0) + value_part, first_row, 0)
        return ((key_acc, value_acc), (query_part * score_scale).astype(jnp.bfloat16))
    start_acc = jnp.zeros((pad_rows + TOKENS, HK, DH), jnp.float32)
    (key_acc, value_acc), query_grads = lax.scan(backward_block, (start_acc, start_acc), block_ids)
    grad_queries = query_grads.reshape(TOKENS, HQ * DH)
    grad_keys = (key_acc[pad_rows:] * score_scale).astype(jnp.bfloat16).reshape(TOKENS, HK * DH)
    grad_values = value_acc[pad_rows:].astype(jnp.bfloat16).reshape(TOKENS, HK * DH)
    return (attn_out, grad_queries, grad_keys, grad_values)
```

```python
import math

import jax
import jax.numpy as jnp
from jax import lax
from jax.experimental import pallas as pl
from jax.experimental.pallas import tpu as pltpu
from jax.sharding import PartitionSpec as P

DH = 128
SPAN = 4
NZ, NY, NX = 8, 4, 4
HEADS = 4
TOK = 256
WIDTH = HEADS * DH
KEYS = (SPAN + 1) * TOK
HALF = NX * WIDTH
CHUNK = 256
SPLIT = WIDTH // CHUNK
ROWS = 2
NEG_FILL = -1e30

MESH = pl.DeviceIdType.MESH
BF = jnp.bfloat16
F32 = jnp.float32
LAST = (((1,), (1,)), ((), ()))
SCALE = 1.0 / math.sqrt(DH)


def aligned(value, step):
    return pl.multiple_of(value * step, step)


def remote(src, dst, send, recv, to):
    return pltpu.make_async_remote_copy(
        src_ref=src, dst_ref=dst, send_sem=send, recv_sem=recv, device_id=to, device_id_type=MESH
    )


def kernel(
    q_hbm, k_hbm, v_hbm, w_ref, og_hbm, len_ref,
    out_hbm, gq_hbm, gk_hbm, gv_hbm,
    q_s, kv_s, vt_s, kt_s, bias_s, s_s, p_s, ctx_s, ctxf_s,
    w_s, wout_s, win_s, g_s, acc_s, gh_s, ds_s, dq_s, delta_s,
    rs_out, rs_in, rs_own, zsum_s, zin_s, attn_s, gq_s,
    dkv_out, dkv_in, dkv_own, gkv_s,
    load_sem, store_sem, sib_sem, kv_ss, kv_rs, z_ss, z_rs, y_ss, y_rs, d_ss, d_rs,
    ox_ss, ox_rs, oz_ss, oz_rs, of_ss, of_rs, rs_ss, rs_rs, rz_ss, rz_rs, gr_ss, gr_rs,
):
    seq = lax.axis_index("seq")
    ten = lax.axis_index("tensor")
    core = lax.rem(seq, 2)
    chip = lax.div(seq, 2)
    y = lax.rem(chip, NY)
    zl = lax.div(chip, NY)
    x = lax.rem(ten, NX)
    zh = lax.div(ten, NX)
    away = 1 - zh
    seqs = 2 * NY * NZ

    def at_x(d):
        return (seq, zh * NX + lax.rem(x + d, NX))

    def at_y(d):
        return ((zl * NY + lax.rem(y + d, NY)) * 2 + core, ten)

    sibling = (chip * 2 + (1 - core), ten)
    partner = (seq, away * NX + x)

    loads = [
        pltpu.make_async_copy(k_hbm, kv_s.at[0, pl.ds(SPAN * TOK, TOK)], load_sem.at[0]),
        pltpu.make_async_copy(v_hbm, kv_s.at[1, pl.ds(SPAN * TOK, TOK)], load_sem.at[1]),
        pltpu.make_async_copy(og_hbm, g_s.at[ten], load_sem.at[2]),
    ] + [
        pltpu.make_async_copy(
            q_hbm.at[:, pl.ds(i * DH, DH)], q_s.at[pl.ds(i * TOK, TOK)], load_sem.at[3 + i]
        )
        for i in range(HEADS)
    ]
    for copy in loads:
        copy.start()

    barrier = pltpu.get_barrier_semaphore()

    def greet(to):
        pl.semaphore_signal(barrier, inc=1, device_id=to, device_id_type=MESH)

    expected = 1 + (NY - 1) + (NX - 1) + 1
    greet(sibling)
    greet(partner)
    for d in range(1, NY):
        greet(at_y(d))
    for d in range(1, NX):
        greet(at_x(d))
    up_ok = zl < NZ - 1
    down_ok = zl > 0

    @pl.when(up_ok)
    def _():
        greet((seq + 2 * NY, ten))

    @pl.when(down_ok)
    def _():
        greet((seq - 2 * NY, ten))

    expected = expected + up_ok.astype(jnp.int32) + down_ok.astype(jnp.int32)
    for d in range(1, SPAN + 1):
        ahead, behind = seq + d < seqs, seq >= d

        @pl.when(ahead)
        def _():
            greet((seq + d, ten))

        @pl.when(behind)
        def _():
            greet((seq - d, ten))

        @pl.when(jnp.logical_not(ahead))
        def _():
            dkv_in[d - 1] = jnp.zeros((2, TOK, DH), BF)

        @pl.when(jnp.logical_not(behind))
        def _():
            kv_s[:, (SPAN - d) * TOK : (SPAN - d + 1) * TOK, :] = jnp.zeros((2, TOK, DH), BF)

        expected = expected + ahead.astype(jnp.int32) + behind.astype(jnp.int32)

    mine = w_ref[:, pl.ds(aligned(core, HALF), HALF)].astype(F32)
    other = w_ref[:, pl.ds(aligned(1 - core, HALF), HALF)].astype(F32)
    wout_s[...] = jnp.concatenate([other[:, : HALF // 2], other[:, HALF // 2 :]], axis=0).astype(BF)

    lengths = len_ref[...]
    docs = lengths.shape[1]
    row = lax.broadcasted_iota(jnp.int32, (docs, docs), 0)
    col = lax.broadcasted_iota(jnp.int32, (docs, docs), 1)
    ends = jnp.sum(jnp.where(col <= row, jnp.broadcast_to(lengths, (docs, docs)), 0), axis=1, keepdims=True)
    place = seq * TOK + lax.broadcasted_iota(jnp.int32, (1, TOK), 1)
    first = jnp.max(jnp.where(ends <= place, ends, 0), axis=0, keepdims=True)
    for e in range(SPAN + 1):
        key_place = (seq - SPAN + e) * TOK + lax.broadcasted_iota(jnp.int32, (TOK, TOK), 0)
        seen = (key_place >= first) & (key_place <= place)
        bias_s[e * TOK : (e + 1) * TOK, :] = jnp.where(seen, 0.0, NEG_FILL)

    pl.semaphore_wait(barrier, expected)

    sib_copy = remote(wout_s, win_s, sib_sem.at[0], sib_sem.at[1], sibling)
    sib_copy.start()

    def kv_copy(d, i, to):
        return remote(
            (k_hbm, v_hbm)[i], kv_s.at[i, pl.ds((SPAN - d) * TOK, TOK)],
            kv_ss.at[d - 1, i], kv_rs.at[d - 1, i], to,
        )

    for d in range(1, SPAN + 1):

        @pl.when(seq + d < seqs)
        def _():
            for i in range(2):
                kv_copy(d, i, (seq + d, ten)).start()

    def ox_copy(d, place):
        return remote(og_hbm, g_s.at[place], ox_ss.at[d - 1], ox_rs.at[d - 1], at_x(d))

    for d in range(1, NX):
        ox_copy(d, ten).start()

    def w_rows(z, yy):
        return w_s.at[core, pl.ds(aligned(z * NY + yy, 16), 16)]

    def z_copy(way, hop, z):
        to = (seq + 2 * NY, ten) if way == 0 else (seq - 2 * NY, ten)
        return remote(w_rows(z, y), w_rows(z, y), z_ss.at[way, hop], z_rs.at[way, hop], to)

    def y_copy(d, z, yy):
        return remote(w_rows(z, yy), w_rows(z, yy), y_ss.at[d - 1, z], y_rs.at[d - 1, z], at_y(d))

    def d_copy(z, half):
        rows = w_s.at[half, pl.ds(aligned(z, NY * 16), NY * 16)]
        return remote(rows, rows, d_ss.at[z], d_rs.at[z], sibling)

    sib_copy.wait_recv()
    came = win_s[...].astype(F32)
    came = jnp.concatenate([came[:8], came[8:]], axis=1)
    upper = jnp.where(core == 0, mine, came)
    lower = jnp.where(core == 0, came, mine)
    w_s[core, pl.ds(aligned(chip, 16), 16), :] = jnp.concatenate([upper, lower], axis=0).astype(BF)

    @pl.when(up_ok)
    def _():
        z_copy(0, 0, zl).start()

    @pl.when(down_ok)
    def _():
        z_copy(1, 0, zl).start()

    for d in range(1, NY):
        y_copy(d, zl, y).start()

    def z_step(hop, carry):
        below, above = zl - hop, zl + hop

        @pl.when(below >= 0)
        def _():
            z_copy(0, hop - 1, below).wait_recv()

            @pl.when(up_ok)
            def _():
                z_copy(0, hop, below).start()

            for d in range(1, NY):
                y_copy(d, below, y).start()

        @pl.when(above < NZ)
        def _():
            z_copy(1, hop - 1, above).wait_recv()

            @pl.when(down_ok)
            def _():
                z_copy(1, hop, above).start()

            for d in range(1, NY):
                y_copy(d, above, y).start()

        return carry

    lax.fori_loop(1, NZ, z_step, 0)

    def oz_copy(i, place):
        rows = pl.ds(i * (TOK // ROWS), TOK // ROWS)
        return remote(og_hbm.at[rows], g_s.at[place, rows], oz_ss.at[i], oz_rs.at[i], partner)

    def of_copy(i, d, place):
        rows = g_s.at[place, pl.ds(i * (TOK // ROWS), TOK // ROWS)]
        return remote(rows, rows, of_ss.at[i, d - 1], of_rs.at[i, d - 1], at_x(d))

    for i in range(ROWS):
        oz_copy(i, ten).start()

    for copy in loads:
        copy.wait()
    for d in range(1, SPAN + 1):

        @pl.when(seq >= d)
        def _():
            for i in range(2):
                kv_copy(d, i, (seq, ten)).wait_recv()

    blocks = [slice(e * TOK, (e + 1) * TOK) for e in range(SPAN + 1)]
    for rows in blocks:
        kt_s[:, rows] = jnp.transpose(kv_s[0, rows, :].astype(F32)).astype(BF)
        vt_s[:, rows] = jnp.transpose(kv_s[1, rows, :].astype(F32)).astype(BF)

    def pass_on(z):
        for d in range(1, NY):
            y_copy(d, z, lax.rem(y + NY - d, NY)).wait_recv()
        d_copy(z, core).start()

    def attend(head, carry):
        lanes = pl.ds(aligned(head, TOK), TOK)
        q = q_s[lanes, :]
        top = jnp.full((1, TOK), NEG_FILL, F32)
        for rows in blocks:
            scores = (
                lax.dot_general(kv_s[0, rows, :], q, LAST, preferred_element_type=F32) * SCALE
                + bias_s[rows, :]
            )
            s_s[rows, :] = scores
            top = jnp.maximum(top, jnp.max(scores, axis=0, keepdims=True))
        total = jnp.zeros((1, TOK), F32)
        for rows in blocks:
            raised = jnp.exp(s_s[rows, :] - top)
            s_s[rows, :] = raised
            total = total + jnp.sum(raised, axis=0, keepdims=True)
        inverse = 1.0 / total
        context = jnp.zeros((DH, TOK), F32)
        for rows in blocks:
            weights = (s_s[rows, :] * inverse).astype(BF)
            p_s[rows, lanes] = weights
            context = context + jnp.dot(vt_s[:, rows], weights, preferred_element_type=F32)
        ctx_s[:, pl.ds(aligned(head, DH), DH)] = jnp.transpose(context).astype(BF)
        for k in (2 * head, 2 * head + 1):

            @pl.when(zl - k >= 0)
            def _():
                pass_on(zl - k)

            @pl.when((k > 0) & (zl + k < NZ))
            def _():
                pass_on(zl + k)

        return carry

    lax.fori_loop(0, HEADS, attend, 0)
    for z in range(NZ):
        d_copy(z, 1 - core).wait_recv()

    def rs_copy(side, place, d):
        return remote(
            rs_out.at[side, place], rs_in.at[side, place],
            rs_ss.at[side, place], rs_rs.at[side, place], at_x(d),
        )

    def share(half, xx, j):
        lanes = pl.ds(aligned(xx * SPLIT + j, CHUNK), CHUNK)
        return jnp.dot(ctx_s[...], w_s[half, :, lanes], preferred_element_type=F32).astype(BF)

    def project(side, half):
        def step(place, carry):
            d, j = lax.rem(place, NX - 1) + 1, lax.div(place, NX - 1)
            rs_out[side, place] = share(half, lax.rem(x + d, NX), j)
            rs_copy(side, place, d).start()
            return carry

        lax.fori_loop(0, SPLIT * (NX - 1), step, 0)

        def own(j, carry):
            rs_own[side, j] = share(half, x, j)
            return carry

        lax.fori_loop(0, SPLIT, own, 0)

    def collect(side, j):
        total = rs_own[side, j].astype(F32)
        for d in range(1, NX):
            place = j * (NX - 1) + d - 1
            rs_copy(side, place, d).wait_recv()
            total = total + rs_in[side, place].astype(F32)
        return total

    project(0, away)

    def rz_copy(j):
        return remote(zsum_s.at[j], zin_s.at[j], rz_ss.at[j], rz_rs.at[j], partner)

    def og_forward(i):
        oz_copy(i, away * NX + x).wait_recv()
        for d in range(1, NX):
            of_copy(i, d, away * NX + x).start()

    project(1, zh)
    og_forward(0)
    for j in range(SPLIT):
        zsum_s[j] = collect(0, j).astype(BF)
        rz_copy(j).start()
    for i in range(1, ROWS):
        og_forward(i)

    def grad_part(half):
        def step(xx, carry):
            lanes = pl.ds(aligned(xx, WIDTH), WIDTH)
            acc_s[...] += lax.dot_general(
                g_s[half * NX + xx], w_s[half, :, lanes], LAST, preferred_element_type=F32
            )
            return carry

        lax.fori_loop(0, NX, step, 0)

    acc_s[...] = jnp.zeros_like(acc_s)
    for d in range(1, NX):
        ox_copy(d, zh * NX + lax.rem(x + NX - d, NX)).wait_recv()
    grad_part(zh)
    for i in range(ROWS):
        for d in range(1, NX):
            of_copy(i, d, away * NX + lax.rem(x + NX - d, NX)).wait_recv()
    grad_part(away)

    for i in range(HEADS):
        grad = acc_s[:, i * DH : (i + 1) * DH].astype(BF)
        gh_s[i * TOK : (i + 1) * TOK, :] = grad
        product = grad.astype(F32) * ctx_s[:, i * DH : (i + 1) * DH].astype(F32)
        delta_s[:, i * TOK : (i + 1) * TOK] = jnp.sum(jnp.transpose(product), axis=0, keepdims=True)

    def gr_copy(d, to):
        return remote(dkv_out.at[d - 1], dkv_in.at[d - 1], gr_ss.at[d - 1], gr_rs.at[d - 1], to)

    dq_s[...] = jnp.zeros_like(dq_s)
    for e, rows in enumerate(blocks):
        d = SPAN - e
        values = kv_s[1, rows, :]

        def back(head, carry):
            lanes = pl.ds(aligned(head, TOK), TOK)
            slope = lax.dot_general(values, gh_s[lanes, :], LAST, preferred_element_type=F32)
            ds_s[:, lanes] = (p_s[rows, lanes].astype(F32) * (slope - delta_s[:, lanes])).astype(BF)
            dq_s[:, lanes] += jnp.dot(kt_s[:, rows], ds_s[:, lanes], preferred_element_type=F32)
            return carry

        lax.fori_loop(0, HEADS, back, 0)
        dk = jnp.dot(ds_s[...], q_s[...], preferred_element_type=F32)
        dv = jnp.dot(p_s[rows, :], gh_s[...], preferred_element_type=F32)
        if d == 0:
            dkv_own[0] = dk
            dkv_own[1] = dv
        else:
            dkv_out[d - 1, 0] = dk.astype(BF)
            dkv_out[d - 1, 1] = dv.astype(BF)

            @pl.when(seq >= d)
            def _():
                gr_copy(d, (seq - d, ten)).start()

    for i in range(HEADS):
        gq_s[:, i * DH : (i + 1) * DH] = (
            jnp.transpose(dq_s[:, i * TOK : (i + 1) * TOK]) * SCALE
        ).astype(BF)
    stores = [pltpu.make_async_copy(gq_s, gq_hbm, store_sem.at[0])]
    stores[0].start()

    for j in range(SPLIT):
        total = collect(1, j)
        rz_copy(j).wait_recv()
        lanes = slice(j * CHUNK, (j + 1) * CHUNK)
        attn_s[:, lanes] = (total + zin_s[j].astype(F32)).astype(BF)
    stores.append(pltpu.make_async_copy(attn_s, out_hbm, store_sem.at[1]))
    stores[1].start()

    for d in range(1, SPAN + 1):

        @pl.when(seq + d < seqs)
        def _():
            gr_copy(d, (seq, ten)).wait_recv()

    for i in range(2):
        total = dkv_own[i]
        for d in range(1, SPAN + 1):
            total = total + dkv_in[d - 1, i].astype(F32)
        gkv_s[i] = ((total * SCALE) if i == 0 else total).astype(BF)
        stores.append(
            pltpu.make_async_copy(gkv_s.at[i], (gk_hbm, gv_hbm)[i], store_sem.at[2 + i])
        )
        stores[-1].start()

    sib_copy.wait_send()
    for d in range(1, SPAN + 1):

        @pl.when(seq + d < seqs)
        def _():
            for i in range(2):
                kv_copy(d, i, (seq, ten)).wait_send()

        @pl.when(seq >= d)
        def _():
            gr_copy(d, (seq, ten)).wait_send()

    for d in range(1, NX):
        ox_copy(d, ten).wait_send()
        for i in range(ROWS):
            of_copy(i, d, away * NX + x).wait_send()
    for i in range(ROWS):
        oz_copy(i, ten).wait_send()

    def drain(z, carry):
        for d in range(1, NY):
            y_copy(d, z, y).wait_send()
        d_copy(z, core).wait_send()

        @pl.when((z <= zl) & up_ok)
        def _():
            z_copy(0, z, zl).wait_send()

        @pl.when((z < NZ - zl) & down_ok)
        def _():
            z_copy(1, z, zl).wait_send()

        return carry

    lax.fori_loop(0, NZ, drain, 0)
    for side in range(2):
        for place in range(SPLIT * (NX - 1)):
            rs_copy(side, place, 1).wait_send()
    for j in range(SPLIT):
        rz_copy(j).wait_send()
    for copy in stores:
        copy.wait()


def local(queries, key_rows, value_rows, out_weight, out_grad, doc_lengths):
    anywhere = pl.BlockSpec(memory_space=pl.ANY)
    vmem = pl.BlockSpec(memory_space=pltpu.VMEM)
    dma = pltpu.SemaphoreType.DMA
    places = SPLIT * (NX - 1)
    scratch = [
        ((HEADS * TOK, DH), BF), ((2, KEYS, DH), BF), ((DH, KEYS), BF), ((DH, KEYS), BF),
        ((KEYS, TOK), F32), ((KEYS, TOK), F32), ((KEYS, HEADS * TOK), BF),
        ((TOK, WIDTH), BF), ((8, 128), F32),
        ((2, WIDTH, HALF), BF), ((16, HALF // 2), BF), ((16, HALF // 2), BF),
        ((2 * NX, TOK, WIDTH), BF), ((TOK, WIDTH), F32), ((HEADS * TOK, DH), BF),
        ((TOK, HEADS * TOK), BF), ((DH, HEADS * TOK), F32), ((1, HEADS * TOK), F32),
        ((2, places, TOK, CHUNK), BF), ((2, places, TOK, CHUNK), BF), ((2, SPLIT, TOK, CHUNK), BF),
        ((SPLIT, TOK, CHUNK), BF), ((SPLIT, TOK, CHUNK), BF), ((TOK, WIDTH), BF), ((TOK, WIDTH), BF),
        ((SPAN, 2, TOK, DH), BF), ((SPAN, 2, TOK, DH), BF), ((2, TOK, DH), F32), ((2, TOK, DH), BF),
    ]
    semaphores = [
        (3 + HEADS,), (4,), (2,), (SPAN, 2), (SPAN, 2), (2, NZ), (2, NZ), (NY - 1, NZ), (NY - 1, NZ),
        (NZ,), (NZ,), (NX - 1,), (NX - 1,), (ROWS,), (ROWS,), (ROWS, NX - 1), (ROWS, NX - 1),
        (2, places), (2, places), (SPLIT,), (SPLIT,), (SPAN,), (SPAN,),
    ]
    return pl.pallas_call(
        kernel,
        name="attention_block",
        out_shape=[
            jax.ShapeDtypeStruct(queries.shape, BF),
            jax.ShapeDtypeStruct(queries.shape, BF),
            jax.ShapeDtypeStruct(key_rows.shape, BF),
            jax.ShapeDtypeStruct(value_rows.shape, BF),
        ],
        in_specs=[anywhere, anywhere, anywhere, vmem, anywhere, vmem],
        out_specs=[anywhere] * 4,
        scratch_shapes=[pltpu.VMEM(shape, kind) for shape, kind in scratch]
        + [dma(shape) for shape in semaphores],
        compiler_params=pltpu.CompilerParams(
            collective_id=0, has_side_effects=True, vmem_limit_bytes=48 * 2**20
        ),
        cost_estimate=pl.CostEstimate(
            flops=5 * 10**9, bytes_accessed=2 * 10**6, transcendentals=1400000
        ),
    )(queries, key_rows, value_rows, out_weight, out_grad, doc_lengths.reshape(1, -1))


def solution(mesh):
    placed = (
        P("seq", "tensor"),
        P("seq", "tensor"),
        P("seq", "tensor"),
        P(("tensor", "seq"), None),
        P("seq", "tensor"),
        P(),
    )
    return jax.shard_map(
        local,
        mesh=mesh,
        in_specs=placed,
        out_specs=(P("seq", "tensor"), P("seq", "tensor"), P("seq", "tensor"), P("seq", "tensor")),
        check_vma=False,
    )
```

```python
import math

import jax
import jax.numpy as jnp
from jax import lax
from jax.experimental import pallas as pl
from jax.experimental.pallas import tpu as pltpu
from jax.sharding import PartitionSpec as P

DH = 128
SPAN = 4
NZ, NY, NX = 8, 4, 4
HEADS = 4
TOK = 256
WIDTH = HEADS * DH
KEYS = (SPAN + 1) * TOK
HALF = NX * WIDTH
CHUNK = 256
SPLIT = WIDTH // CHUNK
PARTS = 8
EARLY = 4
NEG_FILL = -1e30

MESH = pl.DeviceIdType.MESH
BF = jnp.bfloat16
F32 = jnp.float32
LAST = (((1,), (1,)), ((), ()))
SCALE = 1.0 / math.sqrt(DH)


def aligned(value, step):
    return pl.multiple_of(value * step, step)


def remote(src, dst, send, recv, to):
    return pltpu.make_async_remote_copy(
        src_ref=src, dst_ref=dst, send_sem=send, recv_sem=recv, device_id=to, device_id_type=MESH
    )


def kernel(
    q_hbm, k_hbm, v_hbm, w_ref, og_hbm, len_ref,
    out_hbm, gq_hbm, gk_hbm, gv_hbm,
    q_s, kv_s, vt_s, kt_s, bias_s, s_s, p_s, ctx_s,
    w_s, wout_s, win_s, g_s, acc_s, gh_s, ds_s, delta_s,
    rs_out, rs_in, rs_own, zsum_s, zin_s, attn_s, gq_s,
    dkv_out, dkv_in, dkv_own, gkv_s,
    load_sem, store_sem, sib_sem, kv_ss, kv_rs, ks_ss, ks_rs, z_ss, z_rs, y_ss, y_rs, d_ss, d_rs,
    ox_ss, ox_rs, oz_ss, oz_rs, of_ss, of_rs, rs_ss, rs_rs, rz_ss, rz_rs, gr_ss, gr_rs,
):
    seq = lax.axis_index("seq")
    ten = lax.axis_index("tensor")
    core = lax.rem(seq, 2)
    chip = lax.div(seq, 2)
    y = lax.rem(chip, NY)
    zl = lax.div(chip, NY)
    x = lax.rem(ten, NX)
    zh = lax.div(ten, NX)
    away = 1 - zh
    seqs = 2 * NY * NZ

    def at_x(d):
        return (seq, zh * NX + lax.rem(x + d, NX))

    def at_y(d):
        return ((zl * NY + lax.rem(y + d, NY)) * 2 + core, ten)

    sibling = (chip * 2 + (1 - core), ten)
    partner = (seq, away * NX + x)

    loads = [
        pltpu.make_async_copy(k_hbm, kv_s.at[0, pl.ds(SPAN * TOK, TOK)], load_sem.at[0]),
        pltpu.make_async_copy(v_hbm, kv_s.at[1, pl.ds(SPAN * TOK, TOK)], load_sem.at[1]),
        pltpu.make_async_copy(og_hbm, g_s.at[ten], load_sem.at[2]),
    ] + [
        pltpu.make_async_copy(
            q_hbm.at[:, pl.ds(i * DH, DH)], q_s.at[pl.ds(i * TOK, TOK)], load_sem.at[3 + i]
        )
        for i in range(HEADS)
    ]
    for copy in loads:
        copy.start()

    barrier = pltpu.get_barrier_semaphore()

    def greet(to):
        pl.semaphore_signal(barrier, inc=1, device_id=to, device_id_type=MESH)

    expected = 1 + (NY - 1) + (NX - 1) + 1
    greet(sibling)
    greet(partner)
    for d in range(1, NY):
        greet(at_y(d))
    for d in range(1, NX):
        greet(at_x(d))
    up_ok = zl < NZ - 1
    down_ok = zl > 0

    @pl.when(up_ok)
    def _():
        greet((seq + 2 * NY, ten))

    @pl.when(down_ok)
    def _():
        greet((seq - 2 * NY, ten))

    expected = expected + up_ok.astype(jnp.int32) + down_ok.astype(jnp.int32)
    for d in range(1, SPAN + 1):
        ahead, behind = seq + d < seqs, seq >= d

        @pl.when(ahead)
        def _():
            greet((seq + d, ten))

        @pl.when(behind)
        def _():
            greet((seq - d, ten))

        @pl.when(jnp.logical_not(ahead))
        def _():
            dkv_in[d - 1] = jnp.zeros((2, TOK, DH), BF)

        @pl.when(jnp.logical_not(behind))
        def _():
            kv_s[:, (SPAN - d) * TOK : (SPAN - d + 1) * TOK, :] = jnp.zeros((2, TOK, DH), BF)

        expected = expected + ahead.astype(jnp.int32) + behind.astype(jnp.int32)

    mine = w_ref[:, pl.ds(aligned(core, HALF), HALF)].astype(F32)
    other = w_ref[:, pl.ds(aligned(1 - core, HALF), HALF)].astype(F32)
    wout_s[...] = jnp.concatenate([other[:, : HALF // 2], other[:, HALF // 2 :]], axis=0).astype(BF)

    lengths = len_ref[...]
    docs = lengths.shape[1]
    row = lax.broadcasted_iota(jnp.int32, (docs, docs), 0)
    col = lax.broadcasted_iota(jnp.int32, (docs, docs), 1)
    ends = jnp.sum(jnp.where(col <= row, jnp.broadcast_to(lengths, (docs, docs)), 0), axis=1, keepdims=True)
    place = seq * TOK + lax.broadcasted_iota(jnp.int32, (1, TOK), 1)
    first = jnp.max(jnp.where(ends <= place, ends, 0), axis=0, keepdims=True)
    for e in range(SPAN + 1):
        key_place = (seq - SPAN + e) * TOK + lax.broadcasted_iota(jnp.int32, (TOK, TOK), 0)
        seen = (key_place >= first) & (key_place <= place)
        bias_s[e * TOK : (e + 1) * TOK, :] = jnp.where(seen, 0.0, NEG_FILL)

    for copy in loads[:2]:
        copy.wait()
    pl.semaphore_wait(barrier, expected)

    sib_copy = remote(wout_s, win_s, sib_sem.at[0], sib_sem.at[1], sibling)
    sib_copy.start()

    def ox_copy(d, place):
        return remote(og_hbm, g_s.at[place], ox_ss.at[d - 1], ox_rs.at[d - 1], at_x(d))

    for d in range(1, NX):
        ox_copy(d, ten).start()

    def oz_copy(i, place):
        rows = pl.ds(aligned(i, TOK // PARTS), TOK // PARTS)
        return remote(og_hbm.at[rows], g_s.at[place, rows], oz_ss.at[i], oz_rs.at[i], partner)

    def of_copy(i, d, place):
        rows = g_s.at[place, pl.ds(aligned(i, TOK // PARTS), TOK // PARTS)]
        return remote(rows, rows, of_ss.at[i, d - 1], of_rs.at[i, d - 1], at_x(d))

    def og_forward(i, carry=0):
        oz_copy(i, away * NX + x).wait_recv()
        for d in range(1, NX):
            of_copy(i, d, away * NX + x).start()
        return carry

    def kv_rows(e):
        return kv_s.at[:, pl.ds(aligned(e, TOK), TOK)]

    def kv_copy(n, to):
        return remote(kv_rows(SPAN), kv_rows(SPAN - 2 * n), kv_ss.at[n - 1], kv_rs.at[n - 1], to)

    def ks_copy(n):
        return remote(
            kv_rows(SPAN - 2 * n + 2 - 2 * core), kv_rows(SPAN - 2 * n + 1),
            ks_ss.at[n - 1], ks_rs.at[n - 1], sibling,
        )

    def ks_sent(n):
        return seq >= 2 * n - 2 + 2 * core

    def w_rows(z, yy):
        return w_s.at[core, pl.ds(aligned(z * NY + yy, 16), 16)]

    def z_copy(way, hop, z):
        to = (seq + 2 * NY, ten) if way == 0 else (seq - 2 * NY, ten)
        return remote(w_rows(z, y), w_rows(z, y), z_ss.at[way, hop], z_rs.at[way, hop], to)

    def y_copy(d, z, yy):
        return remote(w_rows(z, yy), w_rows(z, yy), y_ss.at[d - 1, z], y_rs.at[d - 1, z], at_y(d))

    def d_copy(z, half):
        rows = w_s.at[half, pl.ds(aligned(z, NY * 16), NY * 16)]
        return remote(rows, rows, d_ss.at[z], d_rs.at[z], sibling)

    sib_copy.wait_recv()
    came = win_s[...].astype(F32)
    came = jnp.concatenate([came[:8], came[8:]], axis=1)
    upper = jnp.where(core == 0, mine, came)
    lower = jnp.where(core == 0, came, mine)
    w_s[core, pl.ds(aligned(chip, 16), 16), :] = jnp.concatenate([upper, lower], axis=0).astype(BF)

    @pl.when(up_ok)
    def _():
        z_copy(0, 0, zl).start()

    @pl.when(down_ok)
    def _():
        z_copy(1, 0, zl).start()

    for d in range(1, NY):
        y_copy(d, zl, y).start()
    for n in range(1, SPAN // 2 + 1):

        @pl.when(seq + 2 * n < seqs)
        def _():
            kv_copy(n, (seq + 2 * n, ten)).start()

    def z_step(hop):
        below, above = zl - hop, zl + hop

        @pl.when(below >= 0)
        def _():
            z_copy(0, hop - 1, below).wait_recv()

            @pl.when(up_ok)
            def _():
                z_copy(0, hop, below).start()

        @pl.when(above < NZ)
        def _():
            z_copy(1, hop - 1, above).wait_recv()

            @pl.when(down_ok)
            def _():
                z_copy(1, hop, above).start()

        @pl.when(below >= 0)
        def _():
            for d in range(1, NY):
                y_copy(d, below, y).start()

        @pl.when(above < NZ)
        def _():
            for d in range(1, NY):
                y_copy(d, above, y).start()

    blocks = [slice(e * TOK, (e + 1) * TOK) for e in range(SPAN + 1)]

    def share_keys():
        for n in range(1, SPAN // 2 + 1):

            @pl.when(seq >= 2 * n)
            def _():
                kv_copy(n, (seq, ten)).wait_recv()

        for n in range(1, SPAN // 2 + 1):

            @pl.when(ks_sent(n))
            def _():
                ks_copy(n).start()

    def turn_keys():
        for n in range(1, SPAN // 2 + 1):

            @pl.when(seq >= 2 * n - 1)
            def _():
                ks_copy(n).wait_recv()

        for rows in blocks:
            kt_s[:, rows] = jnp.transpose(kv_s[0, rows, :].astype(F32)).astype(BF)
            vt_s[:, rows] = jnp.transpose(kv_s[1, rows, :].astype(F32)).astype(BF)

    def attend(heads):
        lanes = [slice(head * TOK, (head + 1) * TOK) for head in heads]
        pair = range(len(heads))
        top = [jnp.full((1, TOK), NEG_FILL, F32)] * len(heads)
        for rows in blocks:
            for u in pair:
                scores = (
                    lax.dot_general(
                        kv_s[0, rows, :], q_s[lanes[u], :], LAST, preferred_element_type=F32
                    )
                    * SCALE
                    + bias_s[rows, :]
                )
                s_s[u, rows, :] = scores
                top[u] = jnp.maximum(top[u], jnp.max(scores, axis=0, keepdims=True))
        total = [jnp.zeros((1, TOK), F32)] * len(heads)
        for rows in blocks:
            for u in pair:
                raised = jnp.exp(s_s[u, rows, :] - top[u])
                s_s[u, rows, :] = raised
                total[u] = total[u] + jnp.sum(raised, axis=0, keepdims=True)
        inverse = [1.0 / each for each in total]
        context = [jnp.zeros((DH, TOK), F32)] * len(heads)
        for rows in blocks:
            for u in pair:
                weights = (s_s[u, rows, :] * inverse[u]).astype(BF)
                p_s[rows, lanes[u]] = weights
                context[u] = context[u] + jnp.dot(
                    vt_s[:, rows], weights, preferred_element_type=F32
                )
        for u in pair:
            ctx_s[:, heads[u] * DH : (heads[u] + 1) * DH] = jnp.transpose(context[u]).astype(BF)

    oz_copy(0, ten).start()
    for hop in range(1, NZ):
        z_step(hop)
        if hop in (2, 4, 6):
            oz_copy(hop // 2, ten).start()
        if hop == 3:
            share_keys()
        if hop == 4:
            for copy in loads[2:]:
                copy.wait()
            turn_keys()
        if hop == 5:
            attend((0, 1))
        if hop == 6:
            attend((2, 3))
    for i in range(EARLY, PARTS):
        oz_copy(i, ten).start()

    def pass_on(z):
        for d in range(1, NY):
            y_copy(d, z, lax.rem(y + NY - d, NY)).wait_recv()
        d_copy(z, core).start()

    def pass_both(k, carry):
        @pl.when(zl - k >= 0)
        def _():
            pass_on(zl - k)

        @pl.when((k > 0) & (zl + k < NZ))
        def _():
            pass_on(zl + k)

        return carry

    lax.fori_loop(0, NZ // 2, pass_both, 0)
    lax.fori_loop(0, EARLY - 1, og_forward, 0)
    lax.fori_loop(NZ // 2, NZ, pass_both, 0)

    def whole():
        for z in range(NZ):
            d_copy(z, 1 - core).wait_recv()

    @pl.when(core != away)
    def _():
        whole()

    def rs_copy(side, place, d):
        return remote(
            rs_out.at[side, place], rs_in.at[side, place],
            rs_ss.at[side, place], rs_rs.at[side, place], at_x(d),
        )

    def share(half, xx, j):
        lanes = pl.ds(aligned(xx * SPLIT + j, CHUNK), CHUNK)
        return jnp.dot(ctx_s[...], w_s[half, :, lanes], preferred_element_type=F32).astype(BF)

    def project(side, half, send):
        for j in range(SPLIT):
            for d in range(1, NX):
                place = j * (NX - 1) + d - 1
                rs_out[side, place] = share(half, lax.rem(x + d, NX), j)
                if send:
                    rs_copy(side, place, d).start()
        for j in range(SPLIT):
            rs_own[side, j] = share(half, x, j)

    def collect(side, j):
        total = rs_own[side, j].astype(F32)
        for d in range(1, NX):
            place = j * (NX - 1) + d - 1
            rs_copy(side, place, d).wait_recv()
            total = total + rs_in[side, place].astype(F32)
        return total

    def rz_copy(j):
        return remote(zsum_s.at[j], zin_s.at[j], rz_ss.at[j], rz_rs.at[j], partner)

    def grad_part(half):
        total = jnp.zeros((TOK, WIDTH), F32)
        for xx in range(NX):
            total = total + lax.dot_general(
                g_s[half * NX + xx], w_s[half, :, xx * WIDTH : (xx + 1) * WIDTH], LAST,
                preferred_element_type=F32,
            )
        return total

    project(0, away, True)

    @pl.when(core == away)
    def _():
        whole()

    project(1, zh, False)
    zsum_s[0] = collect(0, 0).astype(BF)
    rz_copy(0).start()
    for d in range(1, NX):
        ox_copy(d, zh * NX + lax.rem(x + NX - d, NX)).wait_recv()
    acc_s[...] = grad_part(zh)
    lax.fori_loop(EARLY - 1, PARTS - 2, og_forward, 0)
    for j in range(1, SPLIT):
        zsum_s[j] = collect(0, j).astype(BF)
        rz_copy(j).start()
    lax.fori_loop(PARTS - 2, PARTS, og_forward, 0)
    for place in range(SPLIT * (NX - 1)):
        rs_copy(1, place, place % (NX - 1) + 1).start()

    def og_arrived(i, carry):
        for d in range(1, NX):
            of_copy(i, d, away * NX + lax.rem(x + NX - d, NX)).wait_recv()
        return carry

    lax.fori_loop(0, PARTS, og_arrived, 0)
    acc_s[...] += grad_part(away)

    for i in range(HEADS):
        grad = acc_s[:, i * DH : (i + 1) * DH].astype(BF)
        gh_s[i * TOK : (i + 1) * TOK, :] = grad
        product = grad.astype(F32) * ctx_s[:, i * DH : (i + 1) * DH].astype(F32)
        delta_s[:, i * TOK : (i + 1) * TOK] = jnp.sum(jnp.transpose(product), axis=0, keepdims=True)

    def gr_copy(d, to):
        return remote(dkv_out.at[d - 1], dkv_in.at[d - 1], gr_ss.at[d - 1], gr_rs.at[d - 1], to)

    for e, rows in enumerate(blocks):
        d = SPAN - e
        values = kv_s[1, rows, :]
        for head in range(HEADS):
            lanes = slice(head * TOK, (head + 1) * TOK)
            slope = lax.dot_general(values, gh_s[lanes, :], LAST, preferred_element_type=F32)
            ds_s[rows, lanes] = (p_s[rows, lanes].astype(F32) * (slope - delta_s[:, lanes])).astype(BF)
        dk = jnp.dot(ds_s[rows, :], q_s[...], preferred_element_type=F32)
        dv = jnp.dot(p_s[rows, :], gh_s[...], preferred_element_type=F32)
        if d == 0:
            dkv_own[0] = dk
            dkv_own[1] = dv
        else:
            dkv_out[d - 1, 0] = dk.astype(BF)
            dkv_out[d - 1, 1] = dv.astype(BF)

            @pl.when(seq >= d)
            def _():
                gr_copy(d, (seq - d, ten)).start()

    for i in range(HEADS):
        lanes = slice(i * TOK, (i + 1) * TOK)
        dq = jnp.dot(kt_s[...], ds_s[:, lanes], preferred_element_type=F32)
        gq_s[:, i * DH : (i + 1) * DH] = (jnp.transpose(dq) * SCALE).astype(BF)
    stores = [pltpu.make_async_copy(gq_s, gq_hbm, store_sem.at[0])]
    stores[0].start()

    for j in range(SPLIT):
        total = collect(1, j)
        rz_copy(j).wait_recv()
        lanes = slice(j * CHUNK, (j + 1) * CHUNK)
        attn_s[:, lanes] = (total + zin_s[j].astype(F32)).astype(BF)
    stores.append(pltpu.make_async_copy(attn_s, out_hbm, store_sem.at[1]))
    stores[1].start()

    for d in range(1, SPAN + 1):

        @pl.when(seq + d < seqs)
        def _():
            gr_copy(d, (seq, ten)).wait_recv()

    for i in range(2):
        total = dkv_own[i]
        for d in range(1, SPAN + 1):
            total = total + dkv_in[d - 1, i].astype(F32)
        gkv_s[i] = ((total * SCALE) if i == 0 else total).astype(BF)
        stores.append(
            pltpu.make_async_copy(gkv_s.at[i], (gk_hbm, gv_hbm)[i], store_sem.at[2 + i])
        )
        stores[-1].start()

    sib_copy.wait_send()
    for n in range(1, SPAN // 2 + 1):

        @pl.when(seq + 2 * n < seqs)
        def _():
            kv_copy(n, (seq, ten)).wait_send()

        @pl.when(ks_sent(n))
        def _():
            ks_copy(n).wait_send()

    for d in range(1, SPAN + 1):

        @pl.when(seq >= d)
        def _():
            gr_copy(d, (seq, ten)).wait_send()

    for d in range(1, NX):
        ox_copy(d, ten).wait_send()

    def sent(i, carry):
        oz_copy(i, ten).wait_send()
        for d in range(1, NX):
            of_copy(i, d, away * NX + x).wait_send()
        return carry

    lax.fori_loop(0, PARTS, sent, 0)

    def drain(z, carry):
        for d in range(1, NY):
            y_copy(d, z, y).wait_send()
        d_copy(z, core).wait_send()

        @pl.when((z <= zl) & up_ok)
        def _():
            z_copy(0, z, zl).wait_send()

        @pl.when((z < NZ - zl) & down_ok)
        def _():
            z_copy(1, z, zl).wait_send()

        return carry

    lax.fori_loop(0, NZ, drain, 0)
    for side in range(2):
        for place in range(SPLIT * (NX - 1)):
            rs_copy(side, place, 1).wait_send()
    for j in range(SPLIT):
        rz_copy(j).wait_send()
    for copy in stores:
        copy.wait()


def local(queries, key_rows, value_rows, out_weight, out_grad, doc_lengths):
    anywhere = pl.BlockSpec(memory_space=pltpu.HBM)
    vmem = pl.BlockSpec(memory_space=pltpu.VMEM)
    dma = pltpu.SemaphoreType.DMA
    places = SPLIT * (NX - 1)
    scratch = [
        ((HEADS * TOK, DH), BF), ((2, KEYS, DH), BF), ((DH, KEYS), BF), ((DH, KEYS), BF),
        ((KEYS, TOK), F32), ((2, KEYS, TOK), F32), ((KEYS, HEADS * TOK), BF),
        ((TOK, WIDTH), BF),
        ((2, WIDTH, HALF), BF), ((16, HALF // 2), BF), ((16, HALF // 2), BF),
        ((2 * NX, TOK, WIDTH), BF), ((TOK, WIDTH), F32), ((HEADS * TOK, DH), BF),
        ((KEYS, HEADS * TOK), BF), ((1, HEADS * TOK), F32),
        ((2, places, TOK, CHUNK), BF), ((2, places, TOK, CHUNK), BF), ((2, SPLIT, TOK, CHUNK), BF),
        ((SPLIT, TOK, CHUNK), BF), ((SPLIT, TOK, CHUNK), BF), ((TOK, WIDTH), BF), ((TOK, WIDTH), BF),
        ((SPAN, 2, TOK, DH), BF), ((SPAN, 2, TOK, DH), BF), ((2, TOK, DH), F32), ((2, TOK, DH), BF),
    ]
    semaphores = [
        (3 + HEADS,), (4,), (2,), (SPAN // 2,), (SPAN // 2,), (SPAN // 2,), (SPAN // 2,), (2, NZ), (2, NZ), (NY - 1, NZ), (NY - 1, NZ),
        (NZ,), (NZ,), (NX - 1,), (NX - 1,), (PARTS,), (PARTS,), (PARTS, NX - 1), (PARTS, NX - 1),
        (2, places), (2, places), (SPLIT,), (SPLIT,), (SPAN,), (SPAN,),
    ]
    return pl.pallas_call(
        kernel,
        name="attention_block",
        out_shape=[
            jax.ShapeDtypeStruct(queries.shape, BF),
            jax.ShapeDtypeStruct(queries.shape, BF),
            jax.ShapeDtypeStruct(key_rows.shape, BF),
            jax.ShapeDtypeStruct(value_rows.shape, BF),
        ],
        in_specs=[anywhere, anywhere, anywhere, vmem, anywhere, vmem],
        out_specs=[anywhere] * 4,
        scratch_shapes=[pltpu.VMEM(shape, kind) for shape, kind in scratch]
        + [dma(shape) for shape in semaphores],
        compiler_params=pltpu.CompilerParams(
            collective_id=0, has_side_effects=True, vmem_limit_bytes=60 * 2**20
        ),
        cost_estimate=pl.CostEstimate(
            flops=5 * 10**9, bytes_accessed=2 * 10**6, transcendentals=1400000
        ),
    )(queries, key_rows, value_rows, out_weight, out_grad, doc_lengths.reshape(1, -1))


def solution(mesh):
    placed = (
        P("seq", "tensor"),
        P("seq", "tensor"),
        P("seq", "tensor"),
        P(("tensor", "seq"), None),
        P("seq", "tensor"),
        P(),
    )
    return jax.shard_map(
        local,
        mesh=mesh,
        in_specs=placed,
        out_specs=(P("seq", "tensor"), P("seq", "tensor"), P("seq", "tensor"), P("seq", "tensor")),
        check_vma=False,
    )
```

```python
import math

import jax
import jax.numpy as jnp
from jax import lax
from jax.experimental import pallas as pl
from jax.experimental.pallas import tpu as pltpu
from jax.sharding import PartitionSpec as P

DH = 128
SPAN = 4
NZ, NY, NX = 8, 4, 4
HEADS = 4
TOK = 256
WIDTH = HEADS * DH
KEYS = (SPAN + 1) * TOK
HALF = NX * WIDTH
SIDE = HALF // 2
CHUNK = 256
SPLIT = WIDTH // CHUNK
PARTS = 8
EARLY = 4
NEG_FILL = -1e30

MESH = pl.DeviceIdType.MESH
BF = jnp.bfloat16
F32 = jnp.float32
LAST = (((1,), (1,)), ((), ()))
SCALE = 1.0 / math.sqrt(DH)


def aligned(value, step):
    return pl.multiple_of(value * step, step)


def remote(src, dst, send, recv, to):
    return pltpu.make_async_remote_copy(
        src_ref=src, dst_ref=dst, send_sem=send, recv_sem=recv, device_id=to, device_id_type=MESH
    )


def kernel(
    q_hbm, k_hbm, v_hbm, w_ref, og_hbm, len_ref,
    out_hbm, gq_hbm, gk_hbm, gv_hbm,
    q_s, kv_s, vt_s, kt_s, bias_s, s_s, p_s, ctx_s,
    w_s, wout_s, win_s, g_s, acc_s, gh_s, ds_s, delta_s,
    rs_out, rs_in, rs_own, zsum_s, zin_s, attn_s, gq_s,
    dkv_out, dkv_in, dkv_own, gkv_s, odd_out, odd_in, dkv_f,
    load_sem, store_sem, sib_sem, kv_ss, kv_rs, ks_ss, ks_rs, z_ss, z_rs, y_ss, y_rs, d_ss, d_rs, yl_ss, yl_rs, dl_ss, dl_rs,
    ox_ss, ox_rs, oz_ss, oz_rs, of_ss, of_rs, rs_ss, rs_rs, rz_ss, rz_rs, gr_ss, gr_rs, go_ss, go_rs,
):
    seq = lax.axis_index("seq")
    ten = lax.axis_index("tensor")
    core = lax.rem(seq, 2)
    chip = lax.div(seq, 2)
    y = lax.rem(chip, NY)
    zl = lax.div(chip, NY)
    x = lax.rem(ten, NX)
    zh = lax.div(ten, NX)
    away = 1 - zh
    seqs = 2 * NY * NZ

    def at_x(d):
        return (seq, zh * NX + lax.rem(x + d, NX))

    def at_y(d):
        return ((zl * NY + lax.rem(y + d, NY)) * 2 + core, ten)

    sibling = (chip * 2 + (1 - core), ten)
    partner = (seq, away * NX + x)

    loads = [
        pltpu.make_async_copy(k_hbm, kv_s.at[0, pl.ds(SPAN * TOK, TOK)], load_sem.at[0]),
        pltpu.make_async_copy(v_hbm, kv_s.at[1, pl.ds(SPAN * TOK, TOK)], load_sem.at[1]),
        pltpu.make_async_copy(og_hbm, g_s.at[ten], load_sem.at[2]),
    ] + [
        pltpu.make_async_copy(
            q_hbm.at[:, pl.ds(i * DH, DH)], q_s.at[pl.ds(i * TOK, TOK)], load_sem.at[3 + i]
        )
        for i in range(HEADS)
    ]
    for copy in loads:
        copy.start()

    barrier = pltpu.get_barrier_semaphore()

    def greet(to):
        pl.semaphore_signal(barrier, inc=1, device_id=to, device_id_type=MESH)

    expected = 1 + (NY - 1) + (NX - 1) + 1
    greet(sibling)
    greet(partner)
    for d in range(1, NY):
        greet(at_y(d))
    for d in range(1, NX):
        greet(at_x(d))
    up_ok = zl < NZ - 1
    down_ok = zl > 0

    @pl.when(up_ok)
    def _():
        greet((seq + 2 * NY, ten))

    @pl.when(down_ok)
    def _():
        greet((seq - 2 * NY, ten))

    expected = expected + up_ok.astype(jnp.int32) + down_ok.astype(jnp.int32)
    for d in range(1, SPAN + 1):
        @pl.when(seq < d)
        def _():
            kv_s[:, (SPAN - d) * TOK : (SPAN - d + 1) * TOK, :] = jnp.zeros((2, TOK, DH), BF)

    for n in range(1, SPAN // 2 + 1):
        ahead, behind = seq + 2 * n < seqs, seq >= 2 * n

        @pl.when(ahead)
        def _():
            greet((seq + 2 * n, ten))

        @pl.when(behind)
        def _():
            greet((seq - 2 * n, ten))

        @pl.when(jnp.logical_not(ahead))
        def _():
            dkv_in[n - 1] = jnp.zeros((2, TOK, DH), BF)

        expected = expected + ahead.astype(jnp.int32) + behind.astype(jnp.int32)

    def side_of(half, which):
        start = pl.multiple_of(half * HALF + which * SIDE, SIDE)
        return w_ref[:, pl.ds(start, SIDE)].astype(F32)

    mine = [side_of(half, core) for half in range(2)]
    wout_s[...] = jnp.concatenate([side_of(half, 1 - core) for half in range(2)], axis=0).astype(BF)

    lengths = len_ref[...]
    docs = lengths.shape[1]
    row = lax.broadcasted_iota(jnp.int32, (docs, docs), 0)
    col = lax.broadcasted_iota(jnp.int32, (docs, docs), 1)
    ends = jnp.sum(jnp.where(col <= row, jnp.broadcast_to(lengths, (docs, docs)), 0), axis=1, keepdims=True)
    place = seq * TOK + lax.broadcasted_iota(jnp.int32, (1, TOK), 1)
    first = jnp.max(jnp.where(ends <= place, ends, 0), axis=0, keepdims=True)
    for e in range(SPAN + 1):
        key_place = (seq - SPAN + e) * TOK + lax.broadcasted_iota(jnp.int32, (TOK, TOK), 0)
        seen = (key_place >= first) & (key_place <= place)
        bias_s[e * TOK : (e + 1) * TOK, :] = jnp.where(seen, 0.0, NEG_FILL)

    for copy in loads[:2]:
        copy.wait()
    pl.semaphore_wait(barrier, expected)

    sib_copy = remote(wout_s, win_s, sib_sem.at[0], sib_sem.at[1], sibling)
    sib_copy.start()

    def ox_copy(d, place):
        return remote(og_hbm, g_s.at[place], ox_ss.at[d - 1], ox_rs.at[d - 1], at_x(d))

    for d in range(1, NX):
        ox_copy(d, ten).start()

    def oz_copy(i, place):
        rows = pl.ds(aligned(i, TOK // PARTS), TOK // PARTS)
        return remote(og_hbm.at[rows], g_s.at[place, rows], oz_ss.at[i], oz_rs.at[i], partner)

    def of_copy(i, d, place):
        rows = g_s.at[place, pl.ds(aligned(i, TOK // PARTS), TOK // PARTS)]
        return remote(rows, rows, of_ss.at[i, d - 1], of_rs.at[i, d - 1], at_x(d))

    def og_forward(i, carry=0):
        oz_copy(i, away * NX + x).wait_recv()
        for d in range(1, NX):
            of_copy(i, d, away * NX + x).start()
        return carry

    def kv_rows(e):
        return kv_s.at[:, pl.ds(aligned(e, TOK), TOK)]

    def kv_copy(n, to):
        return remote(kv_rows(SPAN), kv_rows(SPAN - 2 * n), kv_ss.at[n - 1], kv_rs.at[n - 1], to)

    def ks_copy(n):
        return remote(
            kv_rows(SPAN - 2 * n + 2 - 2 * core), kv_rows(SPAN - 2 * n + 1),
            ks_ss.at[n - 1], ks_rs.at[n - 1], sibling,
        )

    def ks_sent(n):
        return seq >= 2 * n - 2 + 2 * core

    def send_keys():
        for n in range(1, SPAN // 2 + 1):

            @pl.when(seq + 2 * n < seqs)
            def _():
                kv_copy(n, (seq + 2 * n, ten)).start()

    send_keys()

    def z_copy(way, hop, z, part):
        to = (seq + 2 * NY, ten) if way == 0 else (seq - 2 * NY, ten)
        half = zh if part else away
        rows = w_s.at[half, z, pl.ds(aligned(y, 16), 16), pl.ds(aligned(core, SIDE), SIDE)]
        return remote(rows, rows, z_ss.at[way, hop, part], z_rs.at[way, hop, part], to)

    def y_copy(d, z, yy):
        rows = w_s.at[away, z, pl.ds(aligned(yy, 16), 16), pl.ds(aligned(core, SIDE), SIDE)]
        return remote(rows, rows, y_ss.at[d - 1, z], y_rs.at[d - 1, z], at_y(d))

    def d_copy(z, which):
        rows = w_s.at[away, z, :, pl.ds(aligned(which, SIDE), SIDE)]
        return remote(rows, rows, d_ss.at[z], d_rs.at[z], sibling)

    def y_late(d, yy):
        rows = w_s.at[zh, :, pl.ds(aligned(yy, 16), 16), pl.ds(aligned(core, SIDE), SIDE)]
        return remote(rows, rows, yl_ss.at[d - 1], yl_rs.at[d - 1], at_y(d))

    def d_late(d, which):
        yy = lax.rem(y + NY - d, NY)
        rows = w_s.at[zh, :, pl.ds(aligned(yy, 16), 16), pl.ds(aligned(which, SIDE), SIDE)]
        return remote(rows, rows, dl_ss.at[d], dl_rs.at[d], sibling)

    sib_copy.wait_recv()
    for half in range(2):
        came = win_s[...].astype(F32)[half * 8 : half * 8 + 8]
        upper = jnp.where(core == 0, mine[half], came)
        lower = jnp.where(core == 0, came, mine[half])
        w_s[half, zl, pl.ds(aligned(y, 16), 16), pl.ds(aligned(core, SIDE), SIDE)] = jnp.concatenate(
            [upper, lower], axis=0
        ).astype(BF)

    for part in range(2):

        @pl.when(up_ok)
        def _():
            z_copy(0, 0, zl, part).start()

        @pl.when(down_ok)
        def _():
            z_copy(1, 0, zl, part).start()

    for d in range(1, NY):
        y_copy(d, zl, y).start()

    def z_step(hop, part):
        below, above = zl - hop, zl + hop

        @pl.when(below >= 0)
        def _():
            z_copy(0, hop - 1, below, part).wait_recv()

            @pl.when(up_ok)
            def _():
                z_copy(0, hop, below, part).start()

        @pl.when(above < NZ)
        def _():
            z_copy(1, hop - 1, above, part).wait_recv()

            @pl.when(down_ok)
            def _():
                z_copy(1, hop, above, part).start()

    def y_step(hop):
        below, above = zl - hop, zl + hop

        @pl.when(below >= 0)
        def _():
            for d in range(1, NY):
                y_copy(d, below, y).start()

        @pl.when(above < NZ)
        def _():
            for d in range(1, NY):
                y_copy(d, above, y).start()

    blocks = [slice(e * TOK, (e + 1) * TOK) for e in range(SPAN + 1)]

    def share_keys():
        for n in range(1, SPAN // 2 + 1):

            @pl.when(seq >= 2 * n)
            def _():
                kv_copy(n, (seq, ten)).wait_recv()

        for n in range(1, SPAN // 2 + 1):

            @pl.when(ks_sent(n))
            def _():
                ks_copy(n).start()

    def turn_keys():
        for n in range(1, SPAN // 2 + 1):

            @pl.when(seq >= 2 * n - 1)
            def _():
                ks_copy(n).wait_recv()

        for rows in blocks:
            kt_s[:, rows] = jnp.transpose(kv_s[0, rows, :].astype(F32)).astype(BF)
            vt_s[:, rows] = jnp.transpose(kv_s[1, rows, :].astype(F32)).astype(BF)

    def attend(heads):
        lanes = [slice(head * TOK, (head + 1) * TOK) for head in heads]
        pair = range(len(heads))
        top = [jnp.full((1, TOK), NEG_FILL, F32)] * len(heads)
        for rows in blocks:
            for u in pair:
                scores = (
                    lax.dot_general(
                        kv_s[0, rows, :], q_s[lanes[u], :], LAST, preferred_element_type=F32
                    )
                    * SCALE
                    + bias_s[rows, :]
                )
                s_s[u, rows, :] = scores
                top[u] = jnp.maximum(top[u], jnp.max(scores, axis=0, keepdims=True))
        total = [jnp.zeros((1, TOK), F32)] * len(heads)
        for rows in blocks:
            for u in pair:
                raised = jnp.exp(s_s[u, rows, :] - top[u])
                s_s[u, rows, :] = raised
                total[u] = total[u] + jnp.sum(raised, axis=0, keepdims=True)
        inverse = [1.0 / each for each in total]
        context = [jnp.zeros((DH, TOK), F32)] * len(heads)
        for rows in blocks:
            for u in pair:
                weights = (s_s[u, rows, :] * inverse[u]).astype(BF)
                p_s[rows, lanes[u]] = weights
                context[u] = context[u] + jnp.dot(
                    vt_s[:, rows], weights, preferred_element_type=F32
                )
        for u in pair:
            ctx_s[:, heads[u] * DH : (heads[u] + 1) * DH] = jnp.transpose(context[u]).astype(BF)

    oz_copy(0, ten).start()
    for hop in range(1, NZ):
        z_step(hop, 0)
        y_step(hop)
        if hop > 1:
            z_step(hop - 1, 1)
        if hop in (2, 4, 6):
            oz_copy(hop // 2, ten).start()
    z_step(NZ - 1, 1)
    for i in range(EARLY, PARTS):
        oz_copy(i, ten).start()

    def pass_on(z):
        for d in range(1, NY):
            y_copy(d, z, lax.rem(y + NY - d, NY)).wait_recv()
        d_copy(z, core).start()

    def pass_both(k, carry):
        @pl.when(zl - k >= 0)
        def _():
            pass_on(zl - k)

        @pl.when((k > 0) & (zl + k < NZ))
        def _():
            pass_on(zl + k)

        return carry

    for copy in loads[2:]:
        copy.wait()
    share_keys()
    lax.fori_loop(0, EARLY - 1, og_forward, 0)
    lax.fori_loop(0, NZ // 2, pass_both, 0)
    turn_keys()
    attend((0, 1))
    lax.fori_loop(NZ // 2, NZ - 1, pass_both, 0)
    attend((2, 3))
    lax.fori_loop(NZ - 1, NZ, pass_both, 0)
    for d in range(1, NY):
        y_late(d, y).start()
    d_late(0, core).start()
    for z in range(NZ):
        d_copy(z, 1 - core).wait_recv()

    def rs_copy(side, place, d):
        return remote(
            rs_out.at[side, place], rs_in.at[side, place],
            rs_ss.at[side, place], rs_rs.at[side, place], at_x(d),
        )

    def share(half, xx, j):
        lanes = pl.ds(aligned(xx * SPLIT + j, CHUNK), CHUNK)
        columns = w_s[half, :, :, lanes].reshape(WIDTH, CHUNK)
        return jnp.dot(ctx_s[...], columns, preferred_element_type=F32).astype(BF)

    def project(side, half):
        for j in range(SPLIT):
            for d in range(1, NX):
                place = j * (NX - 1) + d - 1
                rs_out[side, place] = share(half, lax.rem(x + d, NX), j)
                rs_copy(side, place, d).start()
        for j in range(SPLIT):
            rs_own[side, j] = share(half, x, j)

    def collect(side, j):
        total = rs_own[side, j].astype(F32)
        for d in range(1, NX):
            place = j * (NX - 1) + d - 1
            rs_copy(side, place, d).wait_recv()
            total = total + rs_in[side, place].astype(F32)
        return total

    def rz_copy(j):
        return remote(zsum_s.at[j], zin_s.at[j], rz_ss.at[j], rz_rs.at[j], partner)

    def grad_part(half):
        total = jnp.zeros((TOK, WIDTH), F32)
        for xx in range(NX):
            total = total + lax.dot_general(
                g_s[half * NX + xx],
                w_s[half, :, :, xx * WIDTH : (xx + 1) * WIDTH].reshape(WIDTH, WIDTH),
                LAST,
                preferred_element_type=F32,
            )
        return total

    project(0, away)
    zsum_s[0] = collect(0, 0).astype(BF)
    rz_copy(0).start()
    og_forward(EARLY - 1)
    for j in range(1, SPLIT):
        zsum_s[j] = collect(0, j).astype(BF)
        rz_copy(j).start()
    for d in range(1, NY):
        y_late(d, lax.rem(y + NY - d, NY)).wait_recv()
        d_late(d, core).start()
    lax.fori_loop(EARLY, PARTS, og_forward, 0)
    for d in range(NY):
        d_late(d, 1 - core).wait_recv()
    project(1, zh)
    for d in range(1, NX):
        ox_copy(d, zh * NX + lax.rem(x + NX - d, NX)).wait_recv()
    acc_s[...] = grad_part(zh)

    def og_arrived(i, carry):
        for d in range(1, NX):
            of_copy(i, d, away * NX + lax.rem(x + NX - d, NX)).wait_recv()
        return carry

    lax.fori_loop(0, PARTS, og_arrived, 0)
    acc_s[...] += grad_part(away)

    for i in range(HEADS):
        grad = acc_s[:, i * DH : (i + 1) * DH].astype(BF)
        gh_s[i * TOK : (i + 1) * TOK, :] = grad
        product = grad.astype(F32) * ctx_s[:, i * DH : (i + 1) * DH].astype(F32)
        delta_s[:, i * TOK : (i + 1) * TOK] = jnp.sum(jnp.transpose(product), axis=0, keepdims=True)

    def gr_copy(n, to):
        return remote(dkv_out.at[n - 1], dkv_in.at[n - 1], gr_ss.at[n - 1], gr_rs.at[n - 1], to)

    def odd_copy(n):
        return remote(odd_out.at[n], odd_in.at[n], go_ss.at[n], go_rs.at[n], sibling)

    def back(d):
        rows = blocks[SPAN - d]
        values = kv_s[1, rows, :]
        for head in range(HEADS):
            lanes = slice(head * TOK, (head + 1) * TOK)
            slope = lax.dot_general(values, gh_s[lanes, :], LAST, preferred_element_type=F32)
            ds_s[rows, lanes] = (p_s[rows, lanes].astype(F32) * (slope - delta_s[:, lanes])).astype(BF)
        return (
            jnp.dot(ds_s[rows, :], q_s[...], preferred_element_type=F32),
            jnp.dot(p_s[rows, :], gh_s[...], preferred_element_type=F32),
        )

    for n in range(SPAN // 2 - 1, -1, -1):
        for i, part in enumerate(back(2 * n + 1)):
            odd_out[n, i] = part.astype(BF)
        odd_copy(n).start()
    for n in range(SPAN // 2, 0, -1):
        for i, part in enumerate(back(2 * n)):
            dkv_f[n - 1, i] = part
    for n in range(SPAN // 2):
        odd_copy(n).wait_recv()
    for n in range(SPAN // 2, 0, -1):
        for i in range(2):
            from_one = odd_in[n - 1, i].astype(F32)
            from_two = odd_in[n, i].astype(F32) if n < SPAN // 2 else jnp.zeros((TOK, DH), F32)
            dkv_out[n - 1, i] = (dkv_f[n - 1, i] + jnp.where(core == 0, from_two, from_one)).astype(BF)

        @pl.when(seq >= 2 * n)
        def _():
            gr_copy(n, (seq - 2 * n, ten)).start()

    for i, part in enumerate(back(0)):
        dkv_own[i] = part + jnp.where(core == 0, odd_in[0, i].astype(F32), 0.0)

    for i in range(HEADS):
        lanes = slice(i * TOK, (i + 1) * TOK)
        dq = jnp.dot(kt_s[...], ds_s[:, lanes], preferred_element_type=F32)
        gq_s[:, i * DH : (i + 1) * DH] = (jnp.transpose(dq) * SCALE).astype(BF)
    stores = [pltpu.make_async_copy(gq_s, gq_hbm, store_sem.at[0])]
    stores[0].start()

    for j in range(SPLIT):
        total = collect(1, j)
        rz_copy(j).wait_recv()
        lanes = slice(j * CHUNK, (j + 1) * CHUNK)
        attn_s[:, lanes] = (total + zin_s[j].astype(F32)).astype(BF)
    stores.append(pltpu.make_async_copy(attn_s, out_hbm, store_sem.at[1]))
    stores[1].start()

    for n in range(1, SPAN // 2 + 1):

        @pl.when(seq + 2 * n < seqs)
        def _():
            gr_copy(n, (seq, ten)).wait_recv()

    for i in range(2):
        total = dkv_own[i]
        for n in range(1, SPAN // 2 + 1):
            total = total + dkv_in[n - 1, i].astype(F32)
        gkv_s[i] = ((total * SCALE) if i == 0 else total).astype(BF)
        stores.append(
            pltpu.make_async_copy(gkv_s.at[i], (gk_hbm, gv_hbm)[i], store_sem.at[2 + i])
        )
        stores[-1].start()

    sib_copy.wait_send()
    for n in range(1, SPAN // 2 + 1):

        @pl.when(seq + 2 * n < seqs)
        def _():
            kv_copy(n, (seq, ten)).wait_send()

        @pl.when(ks_sent(n))
        def _():
            ks_copy(n).wait_send()

        @pl.when(seq >= 2 * n)
        def _():
            gr_copy(n, (seq, ten)).wait_send()

        odd_copy(n - 1).wait_send()

    for d in range(1, NY):
        y_late(d, y).wait_send()
    for d in range(NY):
        d_late(d, core).wait_send()
    for d in range(1, NX):
        ox_copy(d, ten).wait_send()

    def sent(i, carry):
        oz_copy(i, ten).wait_send()
        for d in range(1, NX):
            of_copy(i, d, away * NX + x).wait_send()
        return carry

    lax.fori_loop(0, PARTS, sent, 0)

    def drain(z, carry):
        for d in range(1, NY):
            y_copy(d, z, y).wait_send()
        d_copy(z, core).wait_send()

        for part in range(2):

            @pl.when((z <= zl) & up_ok)
            def _():
                z_copy(0, z, zl, part).wait_send()

            @pl.when((z < NZ - zl) & down_ok)
            def _():
                z_copy(1, z, zl, part).wait_send()

        return carry

    lax.fori_loop(0, NZ, drain, 0)
    for side in range(2):
        for place in range(SPLIT * (NX - 1)):
            rs_copy(side, place, 1).wait_send()
    for j in range(SPLIT):
        rz_copy(j).wait_send()
    for copy in stores:
        copy.wait()


def write(*refs):
    for i in range(4):
        refs[4 + i][...] = refs[i][...]


def local(queries, key_rows, value_rows, out_weight, out_grad, doc_lengths):
    anywhere = pl.BlockSpec(memory_space=pltpu.HBM)
    vmem = pl.BlockSpec(memory_space=pltpu.VMEM)
    dma = pltpu.SemaphoreType.DMA
    places = SPLIT * (NX - 1)
    scratch = [
        ((HEADS * TOK, DH), BF), ((2, KEYS, DH), BF), ((DH, KEYS), BF), ((DH, KEYS), BF),
        ((KEYS, TOK), F32), ((2, KEYS, TOK), F32), ((KEYS, HEADS * TOK), BF),
        ((TOK, WIDTH), BF),
        ((2, NZ, NY * 16, HALF), BF), ((16, SIDE), BF), ((16, SIDE), BF),
        ((2 * NX, TOK, WIDTH), BF), ((TOK, WIDTH), F32), ((HEADS * TOK, DH), BF),
        ((KEYS, HEADS * TOK), BF), ((1, HEADS * TOK), F32),
        ((2, places, TOK, CHUNK), BF), ((2, places, TOK, CHUNK), BF), ((2, SPLIT, TOK, CHUNK), BF),
        ((SPLIT, TOK, CHUNK), BF), ((SPLIT, TOK, CHUNK), BF), ((TOK, WIDTH), BF), ((TOK, WIDTH), BF),
        ((SPAN // 2, 2, TOK, DH), BF), ((SPAN // 2, 2, TOK, DH), BF), ((2, TOK, DH), F32), ((2, TOK, DH), BF),
        ((SPAN // 2, 2, TOK, DH), BF), ((SPAN // 2, 2, TOK, DH), BF), ((SPAN // 2, 2, TOK, DH), F32),
    ]
    semaphores = [
        (3 + HEADS,), (4,), (2,), (SPAN // 2,), (SPAN // 2,), (SPAN // 2,), (SPAN // 2,), (2, NZ, 2), (2, NZ, 2), (NY - 1, NZ), (NY - 1, NZ),
        (NZ,), (NZ,), (NY - 1,), (NY - 1,), (NY,), (NY,), (NX - 1,), (NX - 1,), (PARTS,), (PARTS,), (PARTS, NX - 1), (PARTS, NX - 1),
        (2, places), (2, places), (SPLIT,), (SPLIT,), (SPAN // 2,), (SPAN // 2,), (SPAN // 2,), (SPAN // 2,),
    ]
    results = pl.pallas_call(
        kernel,
        name="attention_block",
        out_shape=[
            jax.ShapeDtypeStruct(queries.shape, BF),
            jax.ShapeDtypeStruct(queries.shape, BF),
            jax.ShapeDtypeStruct(key_rows.shape, BF),
            jax.ShapeDtypeStruct(value_rows.shape, BF),
        ],
        in_specs=[anywhere, anywhere, anywhere, vmem, anywhere, vmem],
        out_specs=[anywhere] * 4,
        scratch_shapes=[pltpu.VMEM(shape, kind) for shape, kind in scratch]
        + [dma(shape) for shape in semaphores],
        compiler_params=pltpu.CompilerParams(
            collective_id=0, has_side_effects=True, vmem_limit_bytes=60 * 2**20
        ),
        cost_estimate=pl.CostEstimate(
            flops=5 * 10**9, bytes_accessed=2 * 10**6, transcendentals=1400000
        ),
    )(queries, key_rows, value_rows, out_weight, out_grad, doc_lengths.reshape(1, -1))
    return pl.pallas_call(
        write,
        name="write_results",
        out_shape=[jax.ShapeDtypeStruct(each.shape, BF) for each in results],
        in_specs=[vmem] * 4,
        out_specs=[vmem] * 4,
        compiler_params=pltpu.CompilerParams(vmem_limit_bytes=60 * 2**20),
    )(*results)


def solution(mesh):
    placed = (
        P("seq", "tensor"),
        P("seq", "tensor"),
        P("seq", "tensor"),
        P(("tensor", "seq"), None),
        P("seq", "tensor"),
        P(),
    )
    return jax.shard_map(
        local,
        mesh=mesh,
        in_specs=placed,
        out_specs=(P("seq", "tensor"), P("seq", "tensor"), P("seq", "tensor"), P("seq", "tensor")),
        check_vma=False,
    )
```

```python
import math

import jax
import jax.numpy as jnp
from jax import lax
from jax.experimental import pallas as pl
from jax.experimental.pallas import tpu as pltpu
from jax.sharding import PartitionSpec as P

DH = 128
SPAN = 4
NZ, NY, NX = 8, 4, 4
HEADS = 4
TOK = 256
WIDTH = HEADS * DH
KEYS = (SPAN + 1) * TOK
HALF = NX * WIDTH
SIDE = HALF // 2
CHUNK = 256
SPLIT = WIDTH // CHUNK
PARTS = 8
EARLY = 4
NEG_FILL = -1e30

MESH = pl.DeviceIdType.MESH
BF = jnp.bfloat16
F32 = jnp.float32
LAST = (((1,), (1,)), ((), ()))
SCALE = 1.0 / math.sqrt(DH)


def aligned(value, step):
    return pl.multiple_of(value * step, step)


def remote(src, dst, send, recv, to):
    return pltpu.make_async_remote_copy(
        src_ref=src, dst_ref=dst, send_sem=send, recv_sem=recv, device_id=to, device_id_type=MESH
    )


def kernel(
    q_hbm, k_hbm, v_hbm, w_ref, og_hbm, len_ref,
    out_hbm, gq_hbm, gk_hbm, gv_hbm,
    q_s, kv_s, vt_s, kt_s, bias_s, s_s, p_s, ctx_s,
    w_s, wout_s, win_s, g_s, acc_s, gh_s, ds_s, delta_s,
    rs_out, rs_in, rs_own, zsum_s, zin_s, attn_s, gq_s,
    dkv_out, dkv_in, dkv_own, gkv_s, odd_out, odd_in, dkv_f,
    load_sem, store_sem, sib_sem, kv_ss, kv_rs, ks_ss, ks_rs, z_ss, z_rs, y_ss, y_rs, d_ss, d_rs, yl_ss, yl_rs, dl_ss, dl_rs,
    ox_ss, ox_rs, oz_ss, oz_rs, of_ss, of_rs, rs_ss, rs_rs, rz_ss, rz_rs, gr_ss, gr_rs, go_ss, go_rs,
):
    seq = lax.axis_index("seq")
    ten = lax.axis_index("tensor")
    core = lax.rem(seq, 2)
    chip = lax.div(seq, 2)
    y = lax.rem(chip, NY)
    zl = lax.div(chip, NY)
    x = lax.rem(ten, NX)
    zh = lax.div(ten, NX)
    away = 1 - zh
    seqs = 2 * NY * NZ

    def at_x(d):
        return (seq, zh * NX + lax.rem(x + d, NX))

    def at_y(d):
        return ((zl * NY + lax.rem(y + d, NY)) * 2 + core, ten)

    sibling = (chip * 2 + (1 - core), ten)
    partner = (seq, away * NX + x)

    loads = [
        pltpu.make_async_copy(k_hbm, kv_s.at[0, pl.ds(SPAN * TOK, TOK)], load_sem.at[0]),
        pltpu.make_async_copy(v_hbm, kv_s.at[1, pl.ds(SPAN * TOK, TOK)], load_sem.at[1]),
        pltpu.make_async_copy(og_hbm, g_s.at[ten], load_sem.at[2]),
    ] + [
        pltpu.make_async_copy(
            q_hbm.at[:, pl.ds(i * DH, DH)], q_s.at[pl.ds(i * TOK, TOK)], load_sem.at[3 + i]
        )
        for i in range(HEADS)
    ]
    for copy in loads:
        copy.start()

    barrier = pltpu.get_barrier_semaphore()

    def greet(to):
        pl.semaphore_signal(barrier, inc=1, device_id=to, device_id_type=MESH)

    expected = 1 + (NY - 1) + (NX - 1) + 1
    greet(sibling)
    greet(partner)
    for d in range(1, NY):
        greet(at_y(d))
    for d in range(1, NX):
        greet(at_x(d))
    up_ok = zl < NZ - 1
    down_ok = zl > 0

    @pl.when(up_ok)
    def _():
        greet((seq + 2 * NY, ten))

    @pl.when(down_ok)
    def _():
        greet((seq - 2 * NY, ten))

    expected = expected + up_ok.astype(jnp.int32) + down_ok.astype(jnp.int32)
    for d in range(1, SPAN + 1):
        @pl.when(seq < d)
        def _():
            kv_s[:, (SPAN - d) * TOK : (SPAN - d + 1) * TOK, :] = jnp.zeros((2, TOK, DH), BF)

    for n in range(1, SPAN // 2 + 1):
        ahead, behind = seq + 2 * n < seqs, seq >= 2 * n

        @pl.when(ahead)
        def _():
            greet((seq + 2 * n, ten))

        @pl.when(behind)
        def _():
            greet((seq - 2 * n, ten))

        @pl.when(jnp.logical_not(ahead))
        def _():
            dkv_in[n - 1] = jnp.zeros((2, TOK, DH), BF)

        expected = expected + ahead.astype(jnp.int32) + behind.astype(jnp.int32)

    def side_of(half, which):
        start = pl.multiple_of(half * HALF + which * SIDE, SIDE)
        return w_ref[:, pl.ds(start, SIDE)].astype(F32)

    mine = [side_of(half, core) for half in range(2)]
    wout_s[...] = jnp.concatenate([side_of(half, 1 - core) for half in range(2)], axis=0).astype(BF)

    lengths = len_ref[...]
    docs = lengths.shape[1]
    row = lax.broadcasted_iota(jnp.int32, (docs, docs), 0)
    col = lax.broadcasted_iota(jnp.int32, (docs, docs), 1)
    ends = jnp.sum(jnp.where(col <= row, jnp.broadcast_to(lengths, (docs, docs)), 0), axis=1, keepdims=True)
    place = seq * TOK + lax.broadcasted_iota(jnp.int32, (1, TOK), 1)
    first = jnp.max(jnp.where(ends <= place, ends, 0), axis=0, keepdims=True)
    for e in range(SPAN + 1):
        key_place = (seq - SPAN + e) * TOK + lax.broadcasted_iota(jnp.int32, (TOK, TOK), 0)
        seen = (key_place >= first) & (key_place <= place)
        bias_s[e * TOK : (e + 1) * TOK, :] = jnp.where(seen, 0.0, NEG_FILL)

    for copy in loads[:2]:
        copy.wait()
    pl.semaphore_wait(barrier, expected)

    sib_copy = remote(wout_s, win_s, sib_sem.at[0], sib_sem.at[1], sibling)
    sib_copy.start()

    def ox_copy(d, place):
        return remote(og_hbm, g_s.at[place], ox_ss.at[d - 1], ox_rs.at[d - 1], at_x(d))

    for d in range(1, NX):
        ox_copy(d, ten).start()

    def oz_copy(i, place):
        rows = pl.ds(aligned(i, TOK // PARTS), TOK // PARTS)
        return remote(og_hbm.at[rows], g_s.at[place, rows], oz_ss.at[i], oz_rs.at[i], partner)

    def of_copy(i, d, place):
        rows = g_s.at[place, pl.ds(aligned(i, TOK // PARTS), TOK // PARTS)]
        return remote(rows, rows, of_ss.at[i, d - 1], of_rs.at[i, d - 1], at_x(d))

    def og_forward(i, carry=0):
        oz_copy(i, away * NX + x).wait_recv()
        for d in range(1, NX):
            of_copy(i, d, away * NX + x).start()
        return carry

    def kv_rows(e):
        return kv_s.at[:, pl.ds(aligned(e, TOK), TOK)]

    def kv_copy(n, to):
        return remote(kv_rows(SPAN), kv_rows(SPAN - 2 * n), kv_ss.at[n - 1], kv_rs.at[n - 1], to)

    def ks_copy(n):
        return remote(
            kv_rows(SPAN - 2 * n + 2 - 2 * core), kv_rows(SPAN - 2 * n + 1),
            ks_ss.at[n - 1], ks_rs.at[n - 1], sibling,
        )

    def ks_sent(n):
        return seq >= 2 * n - 2 + 2 * core

    def send_keys():
        for n in range(1, SPAN // 2 + 1):

            @pl.when(seq + 2 * n < seqs)
            def _():
                kv_copy(n, (seq + 2 * n, ten)).start()

    send_keys()

    def z_copy(way, hop, z, part):
        to = (seq + 2 * NY, ten) if way == 0 else (seq - 2 * NY, ten)
        half = zh if part else away
        rows = w_s.at[half, z, pl.ds(aligned(y, 16), 16), pl.ds(aligned(core, SIDE), SIDE)]
        return remote(rows, rows, z_ss.at[way, hop, part], z_rs.at[way, hop, part], to)

    def y_copy(d, z, yy):
        rows = w_s.at[away, z, pl.ds(aligned(yy, 16), 16), pl.ds(aligned(core, SIDE), SIDE)]
        return remote(rows, rows, y_ss.at[d - 1, z], y_rs.at[d - 1, z], at_y(d))

    def d_copy(z, which):
        rows = w_s.at[away, z, :, pl.ds(aligned(which, SIDE), SIDE)]
        return remote(rows, rows, d_ss.at[z], d_rs.at[z], sibling)

    def y_late(d, yy):
        rows = w_s.at[zh, :, pl.ds(aligned(yy, 16), 16), pl.ds(aligned(core, SIDE), SIDE)]
        return remote(rows, rows, yl_ss.at[d - 1], yl_rs.at[d - 1], at_y(d))

    def d_late(d, which):
        yy = lax.rem(y + NY - d, NY)
        rows = w_s.at[zh, :, pl.ds(aligned(yy, 16), 16), pl.ds(aligned(which, SIDE), SIDE)]
        return remote(rows, rows, dl_ss.at[d], dl_rs.at[d], sibling)

    sib_copy.wait_recv()
    for half in range(2):
        came = win_s[...].astype(F32)[half * 8 : half * 8 + 8]
        upper = jnp.where(core == 0, mine[half], came)
        lower = jnp.where(core == 0, came, mine[half])
        w_s[half, zl, pl.ds(aligned(y, 16), 16), pl.ds(aligned(core, SIDE), SIDE)] = jnp.concatenate(
            [upper, lower], axis=0
        ).astype(BF)

    for part in range(2):

        @pl.when(up_ok)
        def _():
            z_copy(0, 0, zl, part).start()

        @pl.when(down_ok)
        def _():
            z_copy(1, 0, zl, part).start()

    for d in range(1, NY):
        y_copy(d, zl, y).start()

    def z_step(hop, part):
        below, above = zl - hop, zl + hop

        @pl.when(below >= 0)
        def _():
            z_copy(0, hop - 1, below, part).wait_recv()

            @pl.when(up_ok)
            def _():
                z_copy(0, hop, below, part).start()

        @pl.when(above < NZ)
        def _():
            z_copy(1, hop - 1, above, part).wait_recv()

            @pl.when(down_ok)
            def _():
                z_copy(1, hop, above, part).start()

    def y_step(hop):
        below, above = zl - hop, zl + hop

        @pl.when(below >= 0)
        def _():
            for d in range(1, NY):
                y_copy(d, below, y).start()

        @pl.when(above < NZ)
        def _():
            for d in range(1, NY):
                y_copy(d, above, y).start()

    blocks = [slice(e * TOK, (e + 1) * TOK) for e in range(SPAN + 1)]

    def share_keys():
        for n in range(1, SPAN // 2 + 1):

            @pl.when(seq >= 2 * n)
            def _():
                kv_copy(n, (seq, ten)).wait_recv()

        for n in range(1, SPAN // 2 + 1):

            @pl.when(ks_sent(n))
            def _():
                ks_copy(n).start()

    def turn_keys():
        for n in range(1, SPAN // 2 + 1):

            @pl.when(seq >= 2 * n - 1)
            def _():
                ks_copy(n).wait_recv()

        for rows in blocks:
            kt_s[:, rows] = jnp.transpose(kv_s[0, rows, :].astype(F32)).astype(BF)
            vt_s[:, rows] = jnp.transpose(kv_s[1, rows, :].astype(F32)).astype(BF)

    def attend(heads):
        lanes = [slice(head * TOK, (head + 1) * TOK) for head in heads]
        pair = range(len(heads))
        top = [jnp.full((1, TOK), NEG_FILL, F32)] * len(heads)
        for rows in blocks:
            for u in pair:
                scores = (
                    lax.dot_general(
                        kv_s[0, rows, :], q_s[lanes[u], :], LAST, preferred_element_type=F32
                    )
                    * SCALE
                    + bias_s[rows, :]
                )
                s_s[u, rows, :] = scores
                top[u] = jnp.maximum(top[u], jnp.max(scores, axis=0, keepdims=True))
        total = [jnp.zeros((1, TOK), F32)] * len(heads)
        for rows in blocks:
            for u in pair:
                raised = jnp.exp(s_s[u, rows, :] - top[u])
                s_s[u, rows, :] = raised
                total[u] = total[u] + jnp.sum(raised, axis=0, keepdims=True)
        inverse = [1.0 / each for each in total]
        context = [jnp.zeros((DH, TOK), F32)] * len(heads)
        for rows in blocks:
            for u in pair:
                weights = (s_s[u, rows, :] * inverse[u]).astype(BF)
                p_s[rows, lanes[u]] = weights
                context[u] = context[u] + jnp.dot(
                    vt_s[:, rows], weights, preferred_element_type=F32
                )
        for u in pair:
            ctx_s[:, heads[u] * DH : (heads[u] + 1) * DH] = jnp.transpose(context[u]).astype(BF)

    oz_copy(0, ten).start()
    for hop in range(1, NZ):
        z_step(hop, 0)
        y_step(hop)
        if hop > 1:
            z_step(hop - 1, 1)
        if hop in (2, 3, 4):
            oz_copy(hop - 1, ten).start()
    z_step(NZ - 1, 1)
    for i in range(EARLY, PARTS):
        oz_copy(i, ten).start()

    def pass_on(z):
        for d in range(1, NY):
            y_copy(d, z, lax.rem(y + NY - d, NY)).wait_recv()
        d_copy(z, core).start()

    def pass_both(k, carry):
        @pl.when(zl - k >= 0)
        def _():
            pass_on(zl - k)

        @pl.when((k > 0) & (zl + k < NZ))
        def _():
            pass_on(zl + k)

        return carry

    for copy in loads[2:]:
        copy.wait()
    share_keys()
    lax.fori_loop(0, EARLY - 1, og_forward, 0)
    lax.fori_loop(0, NZ // 2, pass_both, 0)
    turn_keys()
    attend((0, 1))
    lax.fori_loop(NZ // 2, NZ - 1, pass_both, 0)
    attend((2, 3))
    lax.fori_loop(NZ - 1, NZ, pass_both, 0)
    for d in range(1, NY):
        y_late(d, y).start()
    d_late(0, core).start()
    for z in range(NZ):
        d_copy(z, 1 - core).wait_recv()

    def rs_copy(side, place, d):
        return remote(
            rs_out.at[side, place], rs_in.at[side, place],
            rs_ss.at[side, place], rs_rs.at[side, place], at_x(d),
        )

    def share(half, xx, j):
        lanes = pl.ds(aligned(xx * SPLIT + j, CHUNK), CHUNK)
        columns = w_s[half, :, :, lanes].reshape(WIDTH, CHUNK)
        return jnp.dot(ctx_s[...], columns, preferred_element_type=F32).astype(BF)

    def project(side, half):
        for j in range(SPLIT):
            for d in range(1, NX):
                place = j * (NX - 1) + d - 1
                rs_out[side, place] = share(half, lax.rem(x + d, NX), j)
                rs_copy(side, place, d).start()
        for j in range(SPLIT):
            rs_own[side, j] = share(half, x, j)

    def collect(side, j):
        total = rs_own[side, j].astype(F32)
        for d in range(1, NX):
            place = j * (NX - 1) + d - 1
            rs_copy(side, place, d).wait_recv()
            total = total + rs_in[side, place].astype(F32)
        return total

    def rz_copy(j):
        return remote(zsum_s.at[j], zin_s.at[j], rz_ss.at[j], rz_rs.at[j], partner)

    def grad_part(half):
        total = jnp.zeros((TOK, WIDTH), F32)
        for xx in range(NX):
            total = total + lax.dot_general(
                g_s[half * NX + xx],
                w_s[half, :, :, xx * WIDTH : (xx + 1) * WIDTH].reshape(WIDTH, WIDTH),
                LAST,
                preferred_element_type=F32,
            )
        return total

    project(0, away)
    zsum_s[0] = collect(0, 0).astype(BF)
    rz_copy(0).start()
    og_forward(EARLY - 1)
    for j in range(1, SPLIT):
        zsum_s[j] = collect(0, j).astype(BF)
        rz_copy(j).start()
    lax.fori_loop(EARLY, PARTS, og_forward, 0)
    for d in range(1, NY):
        y_late(d, lax.rem(y + NY - d, NY)).wait_recv()
        d_late(d, core).start()
    for d in range(NY):
        d_late(d, 1 - core).wait_recv()
    project(1, zh)
    for d in range(1, NX):
        ox_copy(d, zh * NX + lax.rem(x + NX - d, NX)).wait_recv()
    acc_s[...] = grad_part(zh)

    def og_arrived(i, carry):
        for d in range(1, NX):
            of_copy(i, d, away * NX + lax.rem(x + NX - d, NX)).wait_recv()
        return carry

    lax.fori_loop(0, PARTS, og_arrived, 0)
    acc_s[...] += grad_part(away)

    for i in range(HEADS):
        grad = acc_s[:, i * DH : (i + 1) * DH].astype(BF)
        gh_s[i * TOK : (i + 1) * TOK, :] = grad
        product = grad.astype(F32) * ctx_s[:, i * DH : (i + 1) * DH].astype(F32)
        delta_s[:, i * TOK : (i + 1) * TOK] = jnp.sum(jnp.transpose(product), axis=0, keepdims=True)

    def gr_copy(n, to):
        return remote(dkv_out.at[n - 1], dkv_in.at[n - 1], gr_ss.at[n - 1], gr_rs.at[n - 1], to)

    def odd_copy(n):
        return remote(odd_out.at[n], odd_in.at[n], go_ss.at[n], go_rs.at[n], sibling)

    def back(d):
        rows = blocks[SPAN - d]
        values = kv_s[1, rows, :]
        for head in range(HEADS):
            lanes = slice(head * TOK, (head + 1) * TOK)
            slope = lax.dot_general(values, gh_s[lanes, :], LAST, preferred_element_type=F32)
            ds_s[rows, lanes] = (p_s[rows, lanes].astype(F32) * (slope - delta_s[:, lanes])).astype(BF)
        return (
            jnp.dot(ds_s[rows, :], q_s[...], preferred_element_type=F32),
            jnp.dot(p_s[rows, :], gh_s[...], preferred_element_type=F32),
        )

    for n in range(SPAN // 2 - 1, -1, -1):
        for i, part in enumerate(back(2 * n + 1)):
            odd_out[n, i] = part.astype(BF)
        odd_copy(n).start()
    for n in range(SPAN // 2, 0, -1):
        for i, part in enumerate(back(2 * n)):
            dkv_f[n - 1, i] = part
    for n in range(SPAN // 2):
        odd_copy(n).wait_recv()
    for n in range(SPAN // 2, 0, -1):
        for i in range(2):
            from_one = odd_in[n - 1, i].astype(F32)
            from_two = odd_in[n, i].astype(F32) if n < SPAN // 2 else jnp.zeros((TOK, DH), F32)
            dkv_out[n - 1, i] = (dkv_f[n - 1, i] + jnp.where(core == 0, from_two, from_one)).astype(BF)

        @pl.when(seq >= 2 * n)
        def _():
            gr_copy(n, (seq - 2 * n, ten)).start()

    for i, part in enumerate(back(0)):
        dkv_own[i] = part + jnp.where(core == 0, odd_in[0, i].astype(F32), 0.0)

    for i in range(HEADS):
        lanes = slice(i * TOK, (i + 1) * TOK)
        dq = jnp.dot(kt_s[...], ds_s[:, lanes], preferred_element_type=F32)
        gq_s[:, i * DH : (i + 1) * DH] = (jnp.transpose(dq) * SCALE).astype(BF)
    stores = [pltpu.make_async_copy(gq_s, gq_hbm, store_sem.at[0])]
    stores[0].start()

    for j in range(SPLIT):
        total = collect(1, j)
        rz_copy(j).wait_recv()
        lanes = slice(j * CHUNK, (j + 1) * CHUNK)
        attn_s[:, lanes] = (total + zin_s[j].astype(F32)).astype(BF)
    stores.append(pltpu.make_async_copy(attn_s, out_hbm, store_sem.at[1]))
    stores[1].start()

    for n in range(1, SPAN // 2 + 1):

        @pl.when(seq + 2 * n < seqs)
        def _():
            gr_copy(n, (seq, ten)).wait_recv()

    for i in range(2):
        total = dkv_own[i]
        for n in range(1, SPAN // 2 + 1):
            total = total + dkv_in[n - 1, i].astype(F32)
        gkv_s[i] = ((total * SCALE) if i == 0 else total).astype(BF)
        stores.append(
            pltpu.make_async_copy(gkv_s.at[i], (gk_hbm, gv_hbm)[i], store_sem.at[2 + i])
        )
        stores[-1].start()

    sib_copy.wait_send()
    for n in range(1, SPAN // 2 + 1):

        @pl.when(seq + 2 * n < seqs)
        def _():
            kv_copy(n, (seq, ten)).wait_send()

        @pl.when(ks_sent(n))
        def _():
            ks_copy(n).wait_send()

        @pl.when(seq >= 2 * n)
        def _():
            gr_copy(n, (seq, ten)).wait_send()

        odd_copy(n - 1).wait_send()

    for d in range(1, NY):
        y_late(d, y).wait_send()
    for d in range(NY):
        d_late(d, core).wait_send()
    for d in range(1, NX):
        ox_copy(d, ten).wait_send()

    def sent(i, carry):
        oz_copy(i, ten).wait_send()
        for d in range(1, NX):
            of_copy(i, d, away * NX + x).wait_send()
        return carry

    lax.fori_loop(0, PARTS, sent, 0)

    def drain(z, carry):
        for d in range(1, NY):
            y_copy(d, z, y).wait_send()
        d_copy(z, core).wait_send()

        for part in range(2):

            @pl.when((z <= zl) & up_ok)
            def _():
                z_copy(0, z, zl, part).wait_send()

            @pl.when((z < NZ - zl) & down_ok)
            def _():
                z_copy(1, z, zl, part).wait_send()

        return carry

    lax.fori_loop(0, NZ, drain, 0)
    for side in range(2):
        for place in range(SPLIT * (NX - 1)):
            rs_copy(side, place, 1).wait_send()
    for j in range(SPLIT):
        rz_copy(j).wait_send()
    for copy in stores:
        copy.wait()


def write(*refs):
    for i in range(4):
        refs[4 + i][...] = refs[i][...]


def local(queries, key_rows, value_rows, out_weight, out_grad, doc_lengths):
    anywhere = pl.BlockSpec(memory_space=pltpu.HBM)
    vmem = pl.BlockSpec(memory_space=pltpu.VMEM)
    dma = pltpu.SemaphoreType.DMA
    places = SPLIT * (NX - 1)
    scratch = [
        ((HEADS * TOK, DH), BF), ((2, KEYS, DH), BF), ((DH, KEYS), BF), ((DH, KEYS), BF),
        ((KEYS, TOK), F32), ((2, KEYS, TOK), F32), ((KEYS, HEADS * TOK), BF),
        ((TOK, WIDTH), BF),
        ((2, NZ, NY * 16, HALF), BF), ((16, SIDE), BF), ((16, SIDE), BF),
        ((2 * NX, TOK, WIDTH), BF), ((TOK, WIDTH), F32), ((HEADS * TOK, DH), BF),
        ((KEYS, HEADS * TOK), BF), ((1, HEADS * TOK), F32),
        ((2, places, TOK, CHUNK), BF), ((2, places, TOK, CHUNK), BF), ((2, SPLIT, TOK, CHUNK), BF),
        ((SPLIT, TOK, CHUNK), BF), ((SPLIT, TOK, CHUNK), BF), ((TOK, WIDTH), BF), ((TOK, WIDTH), BF),
        ((SPAN // 2, 2, TOK, DH), BF), ((SPAN // 2, 2, TOK, DH), BF), ((2, TOK, DH), F32), ((2, TOK, DH), BF),
        ((SPAN // 2, 2, TOK, DH), BF), ((SPAN // 2, 2, TOK, DH), BF), ((SPAN // 2, 2, TOK, DH), F32),
    ]
    semaphores = [
        (3 + HEADS,), (4,), (2,), (SPAN // 2,), (SPAN // 2,), (SPAN // 2,), (SPAN // 2,), (2, NZ, 2), (2, NZ, 2), (NY - 1, NZ), (NY - 1, NZ),
        (NZ,), (NZ,), (NY - 1,), (NY - 1,), (NY,), (NY,), (NX - 1,), (NX - 1,), (PARTS,), (PARTS,), (PARTS, NX - 1), (PARTS, NX - 1),
        (2, places), (2, places), (SPLIT,), (SPLIT,), (SPAN // 2,), (SPAN // 2,), (SPAN // 2,), (SPAN // 2,),
    ]
    results = pl.pallas_call(
        kernel,
        name="attention_block",
        out_shape=[
            jax.ShapeDtypeStruct(queries.shape, BF),
            jax.ShapeDtypeStruct(queries.shape, BF),
            jax.ShapeDtypeStruct(key_rows.shape, BF),
            jax.ShapeDtypeStruct(value_rows.shape, BF),
        ],
        in_specs=[anywhere, anywhere, anywhere, vmem, anywhere, vmem],
        out_specs=[anywhere] * 4,
        scratch_shapes=[pltpu.VMEM(shape, kind) for shape, kind in scratch]
        + [dma(shape) for shape in semaphores],
        compiler_params=pltpu.CompilerParams(
            collective_id=0, has_side_effects=True, vmem_limit_bytes=60 * 2**20
        ),
        cost_estimate=pl.CostEstimate(
            flops=5 * 10**9, bytes_accessed=2 * 10**6, transcendentals=1400000
        ),
    )(queries, key_rows, value_rows, out_weight, out_grad, doc_lengths.reshape(1, -1))
    return pl.pallas_call(
        write,
        name="write_results",
        out_shape=[jax.ShapeDtypeStruct(each.shape, BF) for each in results],
        in_specs=[vmem] * 4,
        out_specs=[vmem] * 4,
        compiler_params=pltpu.CompilerParams(vmem_limit_bytes=60 * 2**20),
    )(*results)


def solution(mesh):
    placed = (
        P("seq", "tensor"),
        P("seq", "tensor"),
        P("seq", "tensor"),
        P(("tensor", "seq"), None),
        P("seq", "tensor"),
        P(),
    )
    return jax.shard_map(
        local,
        mesh=mesh,
        in_specs=placed,
        out_specs=(P("seq", "tensor"), P("seq", "tensor"), P("seq", "tensor"), P("seq", "tensor")),
        check_vma=False,
    )
```
